1024 devices in a mesh: dp: 32 (over z_hi, y, core), expert: 32 (over z_lo, x).
Axes of the slice: x: 4, y: 4, z: 32 (z_hi: 4, z_lo: 8; z = z_hi * 8 + z_lo), core: 2. Of those that a mesh axis runs over, the one named last changes fastest.
Arguments:
- tokens: bfloat16 [131072, 2048], P(('dp', 'expert')), may hold values from -6 to 6
- route_ids: int32 [131072, 1], P(('dp', 'expert')), may hold values from 0 to 31; in each aligned block of 128 rows (0 to 127, 128 to 255, ...) at most 5 rows name the same one
- route_gates: float32 [131072, 1], P(('dp', 'expert')), may hold values from 0.2 to 1
- cotangent: bfloat16 [131072, 2048], P(('dp', 'expert')), may hold values from -1.25 to 1.25
- expert_weights: bfloat16 [32, 2048, 1152], P('expert', 'dp'), may hold values from -0.15625 to 0.15625
- master: float32 [32, 2048, 384], P('expert', 'dp'), may hold values from -0.75 to 0.75
- first_moment: float32 [32, 2048, 384], P('expert', 'dp'), may hold values from -6 to 6
- second_moment: float32 [32, 2048, 384], P('expert', 'dp'), may hold values from 0.1 to 2
- old_place: int32 [32], replicated, may hold values from 0 to 31, as said below
- new_place: int32 [32], replicated, may hold values from 0 to 31, as said below
Outputs:
- combined: bfloat16 [131072, 2048], P(('dp', 'expert'))
- gate_grads: float32 [131072, 1], P(('dp', 'expert'))
- expert_grads: float32 [32, 2048, 384], P('expert', 'dp')
- new_master: float32 [32, 2048, 384], P('expert', 'dp')
- new_first: float32 [32, 2048, 384], P('expert', 'dp')
- new_second: float32 [32, 2048, 384], P('expert', 'dp')
The draws below stay inside these ranges and needn't reach their ends.
Inputs may be any that keep to these rules, and one draw needn't show every extreme that they name: `route_ids`: in the rows of one device (aligned blocks of 128 rows) no expert is named more than 5 times, a bound that some block reaches. `old_place`: A permutation of the experts. `new_place`: A permutation of the experts that differs from old_place in exactly 8 entries.
All inputs are finite; a program needn't handle non-finite values.
Results may differ from the reference program's by a relative error of at most 0.018.
Values may be sent and summed in bfloat16 or wider, within the bound.
A program may use at most 32 MiB of HBM per device.

```python
import math
import jax
import jax.numpy as jnp
import numpy as np
from jax import lax

D = 2048
FF = 384
TOP = 1
MOVED = 8
TOK_DEV = 128
EXPERTS = 32
CAP = 5
TOKENS = 131072
N_DP = 32
N_EXPERT = 32


def placements(key):
    shuffled = jax.random.permutation(jax.random.fold_in(key, 11), EXPERTS).astype(jnp.int32)
    picked = jax.random.permutation(jax.random.fold_in(key, 12), EXPERTS)[:MOVED].astype(jnp.int32)
    rotated = jnp.roll(picked, 1)
    changed = shuffled.at[picked].set(shuffled[rotated])
    return (shuffled, changed)


def draw_old_place(key, part):
    shared = placements(key)
    return shared[0]


def draw_new_place(key, part):
    shared = placements(key)
    return shared[1]


def with_spikes(entries, key, source, target, blocks, factor):
    def block_of(axis_at):
        return (jnp.arange(entries.shape[axis_at]) // (entries.shape[axis_at] // blocks)).reshape((-1,) + (1,) * (entries.ndim - 1 - axis_at))

    first = jax.random.permutation(key, blocks)[block_of(target)]
    second = (block_of(target) + blocks // 2) % blocks
    return jnp.where((block_of(source) == first) | (block_of(source) == second), factor * entries, entries)


def level_of(rng, shape, shards, low, largest):
    def one(dim, parts):
        draws = jax.random.uniform(jax.random.fold_in(jax.random.fold_in(rng, 6), dim), (parts,), jnp.float32, low / len(shards), largest / len(shards))
        return jnp.repeat(jnp.exp(draws), shape[dim] // parts).reshape((-1,) + (1,) * (len(shape) - dim - 1))

    loudness = one(*shards[0])
    for cut in shards[1:]:
        loudness = loudness * one(*cut)
    return loudness


def shared_out(key, own, number, rows, count, top, reach, slope):
    sequence = jax.random.permutation(key, count)
    packed, common = portions_of(count, rows * top, reach, slope, True), portions_of(count, rows * top, reach, slope, False)
    places = jnp.arange(count)

    def named(lengths, turn):
        used = int((lengths > 0).sum())
        fixed = max(1, used // 4)
        moved = fixed + (places - fixed + turn * (used - fixed)) % max(1, count - fixed)
        return jnp.zeros((count,), jnp.int32).at[sequence[jnp.where(places < fixed, places, moved)]].set(jnp.asarray(lengths, jnp.int32))

    lengths = jnp.where(number % 4 == 0, named(packed, number // 4), named(common, number - number // 4 - 1))
    mixed = jax.random.permutation(jax.random.fold_in(own, 3), count)
    source_of, receiver = mixed[0:count // 2 * 2:2], mixed[1:count // 2 * 2:2]
    room = jnp.minimum(lengths[source_of] - 1, reach - lengths[receiver]) // 2
    room = jnp.where((source_of == sequence[0]) | (receiver == sequence[0]) | (lengths[receiver] == 0), 0, jnp.maximum(room, 0))
    moved = jax.random.randint(jax.random.fold_in(own, 4), (count // 2,), 0, 1 << 20) % (room + 1)
    lengths = lengths.at[source_of].add(-moved).at[receiver].add(moved)
    items = jnp.searchsorted(jnp.cumsum(lengths), jnp.arange(rows * top), side="right").astype(jnp.int32)
    listing = items.reshape(top, rows).T
    listing = listing[jax.random.permutation(jax.random.fold_in(own, 1), rows)]
    turn = jax.random.randint(jax.random.fold_in(own, 2), (rows, 1), 0, top)
    return jnp.take_along_axis(listing, (jnp.arange(top)[None, :] + turn) % top, axis=1)


def portions_of(number_of, total, limit, lean, full):
    weights = [(1 << 20) // math.isqrt(grade ** lean) + 1 for grade in range(1, number_of + 1)]
    largest = limit if full else min(limit, max(-(-total // number_of), total * weights[0] // sum(weights)))
    least = 1 if total - largest >= number_of - 1 else 0
    holding, rest = [largest] + [least] * (number_of - 1), total - largest - least * (number_of - 1)
    while rest > 0:
        free = [i for i in range(1, number_of) if holding[i] < largest] or [i for i in range(1, number_of) if holding[i] < limit]
        whole, left = sum([weights[i] for i in free]), rest
        for i in free:
            addition = min(limit - holding[i], max(1, left * weights[i] // whole), rest)
            holding[i] = holding[i] + addition
            rest = rest - addition
    return np.array(holding)


def noise(rng, dims, scale, limit, shards=(), kind=jnp.bfloat16):
    result = jax.random.normal(rng, dims, jnp.float32) * scale
    if len(shards) > 0:
        result = level_of(rng, dims, shards, -0.22, 0.18) * result
    return jnp.clip(result, min=-limit, max=limit).astype(kind)


def heavy_noise(key, dims, width, most, split, heavy, kind=jnp.bfloat16):
    drawn = width * jax.random.normal(key, dims, jnp.float32)
    if split:
        drawn = drawn * level_of(key, dims, split, -0.22, 0.18)
    return jnp.clip(with_spikes(drawn, jax.random.fold_in(key, 3), *heavy), -most, most).astype(kind)


def setup_inputs(seed: int = 0) -> dict:
    streams_of = jax.random.split(jax.random.key(seed), 11)
    tokens = noise(streams_of[0], (TOKENS, D), 1.0, 6.0, ((0, 1024),))
    route_ids_keys = jax.random.split(jax.random.fold_in(streams_of[1], 1), TOKENS // TOK_DEV)
    route_ids_turns = jax.random.permutation(jax.random.fold_in(streams_of[1], 3), TOKENS // TOK_DEV)
    route_ids = jax.vmap(lambda own, number: shared_out(jax.random.fold_in(streams_of[1], 2), own, number, TOK_DEV, EXPERTS, TOP, CAP, 2))(route_ids_keys, route_ids_turns).reshape((TOKENS, TOP))
    route_gates = jnp.clip(0.2 + 0.8 * jax.random.uniform(streams_of[2], (TOKENS, TOP), jnp.float32) ** level_of(streams_of[2], (TOKENS, TOP), ((0, 1024),), -0.2, 0.2), 0.2, 1.0)
    cotangent = heavy_noise(streams_of[3], (TOKENS, D), 0.02, 1.25, ((0, 1024),), (0, 1, 1024, 6.0))
    expert_weights = noise(streams_of[4], (EXPERTS, D, 3 * FF), ((D + FF) // 2) ** -0.5, 0.15625, ((0, 32), (1, 32)))
    master = noise(streams_of[5], (EXPERTS, D, FF), 0.05, 0.75, ((0, 32), (1, 32)), jnp.float32)
    first_moment = noise(streams_of[6], (EXPERTS, D, FF), 0.5, 6.0, ((0, 32), (1, 32)), jnp.float32)
    second_moment = jnp.clip(jnp.exp(math.log(2.0) - 2.9957323 * jax.random.uniform(streams_of[7], (EXPERTS, D, FF), jnp.float32) ** level_of(streams_of[7], (EXPERTS, D, FF), ((0, 32), (1, 32)), -0.2, 0.2)), 0.1, 2.0)
    old_place = draw_old_place(jax.random.fold_in(streams_of[10], 71), 0)
    new_place = draw_new_place(jax.random.fold_in(streams_of[10], 71), 0)
    return {"tokens": tokens, "route_ids": route_ids, "route_gates": route_gates, "cotangent": cotangent, "expert_weights": expert_weights, "master": master, "first_moment": first_moment, "second_moment": second_moment, "old_place": old_place, "new_place": new_place}


beta_first = 0.9
beta_second = 0.999
learn_rate = 0.01
adam_eps = 1e-08

def silu_value(values):
    return values * jax.nn.sigmoid(values)

def contract_rows(left, right):
    return lax.dot_general(left, right, (((0,), (0,)), ((), ())), preferred_element_type=jnp.float32)

def expert_pass(weight, rows_in, rows_up):
    w_gate = weight[:, :FF]
    w_up = weight[:, FF:2 * FF]
    w_down = weight[:, 2 * FF:]
    gate_val = jnp.dot(rows_in, w_gate, preferred_element_type=jnp.float32)
    up_val = jnp.dot(rows_in, w_up, preferred_element_type=jnp.float32)
    hidden = (silu_value(gate_val) * up_val).astype(jnp.bfloat16)
    outputs = lax.dot_general(hidden, w_down, (((1,), (1,)), ((), ())), preferred_element_type=jnp.float32).astype(jnp.bfloat16)
    partial_value = contract_rows(rows_up, hidden)
    return (outputs, partial_value.astype(jnp.bfloat16))

def reference(tokens, route_ids, route_gates, cotangent, expert_weights, master, first_moment, second_moment, old_place, new_place):
    blocks = N_DP * N_EXPERT
    pairs = TOK_DEV * TOP
    expert_range = jnp.arange(EXPERTS, dtype=jnp.int32)
    holder = lax.optimization_barrier(jnp.sum(expert_range[None, :] * (old_place[None, :] == expert_range[:, None]).astype(jnp.int32), axis=1))
    chosen = route_ids.reshape(blocks, pairs)
    onehot = (chosen[:, :, None] == expert_range[None, None, :]).astype(jnp.int32)
    rank_in = lax.optimization_barrier(jnp.sum((jnp.cumsum(onehot, axis=1) - onehot) * onehot, axis=2))
    target = jnp.take(holder, chosen)
    source = (jnp.arange(blocks, dtype=jnp.int32) % N_EXPERT)[:, None]
    position = (source * CAP + rank_in).astype(jnp.int32)
    group_target = target.reshape(N_DP, N_EXPERT * pairs)
    group_position = position.reshape(N_DP, N_EXPERT * pairs)
    group_tokens = tokens.reshape(N_DP, N_EXPERT * TOK_DEV, D)
    group_gates = route_gates.reshape(N_DP, N_EXPERT * TOK_DEV, TOP)
    group_cot = cotangent.reshape(N_DP, N_EXPERT * TOK_DEV, D)

    def one_group(total, inputs):
        slot_target, slot_position, tokens_here, gates_here, cot_here = inputs
        rows_in = jnp.repeat(tokens_here, TOP, axis=0)
        scaled = (gates_here[:, :, None] * cot_here[:, None, :].astype(jnp.float32)).astype(jnp.bfloat16)
        rows_up = scaled.reshape(N_EXPERT * pairs, D)
        empty = jnp.zeros((EXPERTS, N_EXPERT * CAP, D), jnp.bfloat16)
        buffer_in = empty.at[slot_target, slot_position].set(rows_in)
        buffer_up = empty.at[slot_target, slot_position].set(rows_up)
        outputs, partials = lax.map(lambda items: expert_pass(items[0], items[1], items[2]), (expert_weights, buffer_in, buffer_up))
        picked = outputs[slot_target, slot_position].reshape(N_EXPERT * TOK_DEV, TOP, D).astype(jnp.float32)
        mixed = lax.optimization_barrier(jnp.sum(gates_here[:, :, None] * picked, axis=1)).astype(jnp.bfloat16)
        gate_grad = lax.optimization_barrier(jnp.sum(cot_here[:, None, :].astype(jnp.float32) * picked, axis=2))
        return (total + partials.astype(jnp.float32), (mixed, gate_grad))
    zeros = jnp.zeros((EXPERTS, D, FF), jnp.float32)
    grads, (mixed, gate_grad) = lax.scan(one_group, zeros, (group_target, group_position, group_tokens, group_gates, group_cot))
    combined = mixed.reshape(TOKENS, D)
    gate_grads = gate_grad.reshape(TOKENS, TOP)
    first = beta_first * first_moment + (1.0 - beta_first) * grads
    second = beta_second * second_moment + (1.0 - beta_second) * grads * grads
    updated = master - learn_rate * first / (jnp.sqrt(second) + adam_eps)
    source_slot = lax.optimization_barrier(jnp.sum(expert_range[None, :] * (old_place[None, :] == new_place[:, None]).astype(jnp.int32), axis=1))
    return (combined, gate_grads, grads, jnp.take(updated, source_slot, axis=0), jnp.take(first, source_slot, axis=0), jnp.take(second, source_slot, axis=0))
```

```python
import functools

import jax
import jax.numpy as jnp
from jax import lax
from jax.experimental import pallas as pl
from jax.experimental.pallas import tpu as pltpu
from jax.sharding import PartitionSpec as P

beta_first = 0.9
beta_second = 0.999
learn_rate = 0.01
adam_eps = 1e-08

MESH = pl.DeviceIdType.MESH
ANY = pl.BlockSpec(memory_space=pl.ANY)
VMEM = pl.BlockSpec(memory_space=pltpu.VMEM)
RING = 4
CORES = 2


def silu_value(values):
    return values * jax.nn.sigmoid(values)


def contract_rows(left, right):
    return lax.dot_general(
        left, right, (((0,), (0,)), ((), ())), preferred_element_type=jnp.float32
    )


def place():
    dp, ex = lax.axis_index("dp"), lax.axis_index("expert")
    return dp, ex, dp // (RING * CORES), (dp // CORES) % RING, dp % CORES


def index_of(z, y, core):
    return ((z % RING) * RING + y % RING) * CORES + core


def send(src, dst, send_sem, recv_sem, device):
    return pltpu.make_async_remote_copy(
        src_ref=src,
        dst_ref=dst,
        send_sem=send_sem,
        recv_sem=recv_sem,
        device_id=device,
        device_id_type=MESH,
    )


def greet(devices, experts, dp, ex):
    barrier = pltpu.get_barrier_semaphore()
    for device in devices:
        pl.semaphore_signal(barrier, inc=1, device_id=device, device_id_type=MESH)

    def one(step, carry):
        pl.semaphore_signal(
            barrier, inc=1, device_id=(dp, (ex + step) % experts), device_id_type=MESH
        )
        return carry

    lax.fori_loop(1, experts, one, 0)
    pl.semaphore_wait(barrier, len(devices) + experts - 1)


def exchange(experts, dp, ex, src, dst, send_sems, recv_sems):
    def copy(step):
        target = (ex + step) % experts
        return send(
            src.at[target], dst.at[ex], send_sems.at[target], recv_sems.at[ex], (dp, target)
        )

    def start(step, carry):
        copy(step).start()
        return carry

    def finish(step, carry):
        other = (ex + step) % experts
        send(
            src.at[other], dst.at[other], send_sems.at[other], recv_sems.at[other], (dp, other)
        ).wait()
        return carry

    lax.fori_loop(1, experts, start, 0)
    return lambda: lax.fori_loop(1, experts, finish, 0)


def dispatch_kernel(
    experts,
    weight_ref,
    in_ref,
    up_ref,
    whole_ref,
    recv_in_ref,
    recv_up_ref,
    local_sems,
    in_send,
    in_recv,
    up_send,
    up_recv,
    z_send,
    z_recv,
    y_send,
    y_recv,
    c_send,
    c_recv,
):
    dp, ex, z, y, core = place()
    half = weight_ref.shape[0] // 2
    right, left = (index_of(z + 1, y, core), ex), (index_of(z + 3, y, core), ex)
    sibling = (index_of(z, y, 1 - core), ex)
    ring_y = [(index_of(z, y + s, core), ex) for s in range(1, RING)]
    greet([right, left, sibling] + ring_y, experts, dp, ex)

    own = [
        pltpu.make_async_copy(weight_ref, whole_ref.at[dp], local_sems.at[0]),
        pltpu.make_async_copy(in_ref.at[ex], recv_in_ref.at[ex], local_sems.at[1]),
        pltpu.make_async_copy(up_ref.at[ex], recv_up_ref.at[ex], local_sems.at[2]),
    ]
    for copy in own:
        copy.start()

    sent = []

    def start(copy):
        copy.start()
        sent.append(copy)

    blocks = [dp, left[0], right[0], index_of(z + 2, y, core)]
    low, high = pl.ds(0, half), pl.ds(half, half)

    def z_copy(i, src, index, part, device):
        return send(src, whole_ref.at[index, part], z_send.at[i], z_recv.at[i], device)

    def z_arrival(i, index, part):
        there = whole_ref.at[index, part]
        return send(there, there, z_send.at[i], z_recv.at[i], right)

    whole = pl.ds(0, 2 * half)
    start(z_copy(0, weight_ref, dp, whole, right))
    start(z_copy(1, weight_ref, dp, whole, left))

    def spread(k, src):
        for s in range(1, RING):
            start(
                send(
                    src,
                    whole_ref.at[blocks[k]],
                    y_send.at[k, s - 1],
                    y_recv.at[k, s - 1],
                    ring_y[s - 1],
                )
            )
        start(send(src, whole_ref.at[blocks[k]], c_send.at[k, 0], c_recv.at[k, 0], sibling))

    def pass_on(k):
        for s in range(1, RING):
            index = index_of(blocks[k] // (RING * CORES), y + RING - s, core)
            there = whole_ref.at[index]
            send(there, there, y_send.at[k, s - 1], y_recv.at[k, s - 1], sibling).wait_recv()
            start(send(there, there, c_send.at[k, s], c_recv.at[k, s], sibling))

    spread(0, weight_ref)
    finish_in = exchange(experts, dp, ex, in_ref, recv_in_ref, in_send, in_recv)
    finish_up = exchange(experts, dp, ex, up_ref, recv_up_ref, up_send, up_recv)
    z_arrival(0, blocks[1], whole).wait_recv()
    start(z_copy(2, whole_ref.at[blocks[1], low], blocks[1], low, right))
    spread(1, whole_ref.at[blocks[1]])
    z_arrival(1, blocks[2], whole).wait_recv()
    start(z_copy(3, whole_ref.at[blocks[2], high], blocks[2], high, left))
    spread(2, whole_ref.at[blocks[2]])
    pass_on(0)
    z_arrival(2, blocks[3], low).wait_recv()
    z_arrival(3, blocks[3], high).wait_recv()
    spread(3, whole_ref.at[blocks[3]])
    pass_on(1)
    pass_on(2)
    pass_on(3)
    for k in range(RING):
        for s in range(RING):
            index = index_of(blocks[k] // (RING * CORES), y + RING - s, 1 - core)
            there = whole_ref.at[index]
            send(there, there, c_send.at[k, s], c_recv.at[k, s], sibling).wait_recv()
    for copy in sent:
        copy.wait_send()
    finish_in()
    finish_up()
    for copy in own:
        copy.wait()


def dispatch(weight, send_in, send_up, devices):
    experts = send_in.shape[0]
    dma = pltpu.SemaphoreType.DMA
    return pl.pallas_call(
        functools.partial(dispatch_kernel, experts),
        out_shape=[
            jax.ShapeDtypeStruct((devices,) + weight.shape, weight.dtype),
            jax.ShapeDtypeStruct(send_in.shape, send_in.dtype),
            jax.ShapeDtypeStruct(send_up.shape, send_up.dtype),
        ],
        in_specs=[ANY] * 3,
        out_specs=[ANY] * 3,
        scratch_shapes=[dma((3,))]
        + [dma((experts,))] * 4
        + [dma((RING,))] * 2
        + [dma((RING, RING - 1))] * 2
        + [dma((RING, RING))] * 2,
        compiler_params=pltpu.CompilerParams(collective_id=0, has_side_effects=True),
        name="dispatch",
    )(weight, send_in, send_up)


def give_back_kernel(
    experts,
    out_ref,
    partial_ref,
    returned_ref,
    grads_ref,
    c_buf,
    y_from,
    y_buf,
    z_from,
    z_buf,
    local_sem,
    out_send,
    out_recv,
    c_send,
    c_recv,
    y_send,
    y_recv,
    z_send,
    z_recv,
):
    dp, ex, z, y, core = place()
    sibling = (index_of(z, y, 1 - core), ex)
    ring_y = [(index_of(z, y + s, core), ex) for s in range(1, RING)]
    ring_z = [(index_of(z + s, y, core), ex) for s in range(1, RING)]
    greet([sibling] + ring_y + ring_z, experts, dp, ex)

    to_core = send(partial_ref.at[:, :, 1 - core], c_buf, c_send, c_recv, sibling)
    to_core.start()
    own = pltpu.make_async_copy(out_ref.at[ex], returned_ref.at[ex], local_sem)
    own.start()
    finish_out = exchange(experts, dp, ex, out_ref, returned_ref, out_send, out_recv)
    to_core.wait()

    def pair(i, carry):
        at, row = i // RING, i % RING
        y_from[row, at] = (
            partial_ref[at, row, core].astype(jnp.float32) + c_buf[at, row].astype(jnp.float32)
        ).astype(y_from.dtype)
        return carry

    lax.fori_loop(0, RING * RING, pair, 0)
    y_copies = [
        send(
            y_from.at[(y + s) % RING],
            y_buf.at[s - 1],
            y_send.at[s - 1],
            y_recv.at[s - 1],
            ring_y[s - 1],
        )
        for s in range(1, RING)
    ]
    for copy in y_copies:
        copy.start()
    for copy in y_copies:
        copy.wait()

    def quad(i, carry):
        total = y_from[y, i].astype(jnp.float32)
        for s in range(RING - 1):
            total += y_buf[s, i].astype(jnp.float32)
        z_from[i] = total.astype(z_from.dtype)
        return carry

    lax.fori_loop(0, RING, quad, 0)
    z_copies = [
        send(
            z_from.at[(z + s) % RING],
            z_buf.at[s - 1],
            z_send.at[s - 1],
            z_recv.at[s - 1],
            ring_z[s - 1],
        )
        for s in range(1, RING)
    ]
    for copy in z_copies:
        copy.start()
    for copy in z_copies:
        copy.wait()
    total = z_from[z].astype(jnp.float32)
    for s in range(RING - 1):
        total += z_buf[s].astype(jnp.float32)
    grads_ref[...] = total
    finish_out()
    own.wait()


def give_back(outputs, partial):
    experts = outputs.shape[0]
    dma = pltpu.SemaphoreType.DMA
    rows, width = partial.shape[3:]
    block = (rows, width)
    return pl.pallas_call(
        functools.partial(give_back_kernel, experts),
        out_shape=[
            jax.ShapeDtypeStruct(outputs.shape, outputs.dtype),
            jax.ShapeDtypeStruct(block, jnp.float32),
        ],
        in_specs=[ANY, VMEM],
        out_specs=[ANY, VMEM],
        scratch_shapes=[
            pltpu.VMEM((RING, RING) + block, partial.dtype),
            pltpu.VMEM((RING, RING) + block, partial.dtype),
            pltpu.VMEM((RING - 1, RING) + block, partial.dtype),
            pltpu.VMEM((RING,) + block, partial.dtype),
            pltpu.VMEM((RING - 1,) + block, partial.dtype),
            dma,
            dma((experts,)),
            dma((experts,)),
            dma,
            dma,
        ]
        + [dma((RING - 1,))] * 4,
        compiler_params=pltpu.CompilerParams(
            collective_id=1, has_side_effects=True, vmem_limit_bytes=24 * 1024 * 1024
        ),
        name="give_back",
    )(outputs, partial)


def shards(
    tokens,
    route_ids,
    route_gates,
    cotangent,
    expert_weights,
    master,
    first_moment,
    second_moment,
    old_place,
    new_place,
):
    experts = lax.axis_size("expert")
    devices = lax.axis_size("dp")
    tok_rows, model = tokens.shape
    routes = route_ids.shape[1]
    capacity = 5 * tok_rows * routes // (4 * experts)
    slots = experts * capacity
    ff_width = expert_weights.shape[2] // 3
    expert_range = jnp.arange(experts, dtype=jnp.int32)
    holder = jnp.sum(
        expert_range[None, :] * (old_place[None, :] == expert_range[:, None]).astype(jnp.int32),
        axis=1,
    )
    flat_ids = route_ids.reshape(-1)
    onehot = (flat_ids[:, None] == expert_range[None, :]).astype(jnp.int32)
    rank_in = jnp.sum((jnp.cumsum(onehot, axis=0) - onehot) * onehot, axis=1)
    target = jnp.sum(onehot * holder[None, :], axis=1)
    slot_index = target * capacity + rank_in
    slot_range = jnp.arange(slots, dtype=jnp.int32)
    place_pairs = (slot_range[:, None] == slot_index[None, :]).astype(jnp.bfloat16)
    place_tokens = jnp.sum(place_pairs.reshape(slots, tok_rows, routes), axis=2)
    send_in = jnp.dot(place_tokens, tokens, preferred_element_type=jnp.float32).astype(jnp.bfloat16)
    scaled = (route_gates[:, :, None] * cotangent[:, None, :].astype(jnp.float32)).astype(
        jnp.bfloat16
    )
    send_up = jnp.dot(
        place_pairs, scaled.reshape(tok_rows * routes, -1), preferred_element_type=jnp.float32
    ).astype(jnp.bfloat16)
    packed = (experts, capacity * model // 128, 128)
    weight, recv_in, recv_up = dispatch(
        expert_weights[0], send_in.reshape(packed), send_up.reshape(packed), devices
    )
    weight = weight.reshape(model, -1)
    recv_in = recv_in.reshape(slots, model)
    recv_up = recv_up.reshape(slots, model)
    gate_val = jnp.dot(recv_in, weight[:, :ff_width], preferred_element_type=jnp.float32)
    up_val = jnp.dot(
        recv_in, weight[:, ff_width : 2 * ff_width], preferred_element_type=jnp.float32
    )
    hidden = (silu_value(gate_val) * up_val).astype(jnp.bfloat16)
    outputs = lax.dot_general(
        hidden,
        weight[:, 2 * ff_width :],
        (((1,), (1,)), ((), ())),
        preferred_element_type=jnp.float32,
    ).astype(jnp.bfloat16)
    partial = contract_rows(recv_up, hidden).astype(jnp.bfloat16)
    returned, grads = give_back(
        outputs.reshape(packed), partial.reshape(RING, RING, CORES, -1, ff_width)
    )
    returned = returned.reshape(slots, model)
    picked = (
        jnp.take(returned, slot_index, axis=0).reshape(tok_rows, routes, -1).astype(jnp.float32)
    )
    combined = jnp.sum(route_gates[:, :, None] * picked, axis=1).astype(jnp.bfloat16)
    gate_grads = jnp.sum(cotangent[:, None, :].astype(jnp.float32) * picked, axis=2)
    grads = grads[None]
    first = beta_first * first_moment + (1.0 - beta_first) * grads
    second = beta_second * second_moment + (1.0 - beta_second) * grads * grads
    updated = master - learn_rate * first / (jnp.sqrt(second) + adam_eps)
    source_slot = jnp.sum(
        expert_range[None, :] * (old_place[None, :] == new_place[:, None]).astype(jnp.int32), axis=1
    )
    state = jnp.concatenate([updated, first, second], axis=2).astype(jnp.bfloat16)
    rows = state.shape[1]
    state = state.reshape(experts, rows // experts, -1)
    spread = lax.all_to_all(state, "expert", split_axis=0, concat_axis=0, tiled=True)
    ordered = jnp.take(spread, source_slot, axis=0)
    moved = lax.all_to_all(ordered, "expert", split_axis=0, concat_axis=0, tiled=True)
    moved = moved.reshape(1, rows, 3, ff_width).astype(jnp.float32)
    return (combined, gate_grads, grads, moved[:, :, 0], moved[:, :, 1], moved[:, :, 2])


def solution(mesh):
    in_specs = (
        P(("dp", "expert"), None),
        P(("dp", "expert"), None),
        P(("dp", "expert"), None),
        P(("dp", "expert"), None),
        P("expert", "dp", None),
        P("expert", "dp", None),
        P("expert", "dp", None),
        P("expert", "dp", None),
        P(),
        P(),
    )
    out_specs = (
        P(("dp", "expert"), None),
        P(("dp", "expert"), None),
        P("expert", "dp", None),
        P("expert", "dp", None),
        P("expert", "dp", None),
        P("expert", "dp", None),
    )
    return jax.shard_map(shards, mesh=mesh, in_specs=in_specs, out_specs=out_specs, check_vma=False)
```

```python
import functools

import jax
import jax.numpy as jnp
from jax import lax
from jax.experimental import pallas as pl
from jax.experimental.pallas import tpu as pltpu
from jax.sharding import PartitionSpec as P

beta_first = 0.9
beta_second = 0.999
learn_rate = 0.01
adam_eps = 1e-08

MESH = pl.DeviceIdType.MESH
ANY = pl.BlockSpec(memory_space=pl.ANY)
VMEM = pl.BlockSpec(memory_space=pltpu.VMEM)
RING = 4
CORES = 2


def silu_value(values):
    return values * jax.nn.sigmoid(values)


def contract_rows(left, right):
    return lax.dot_general(
        left, right, (((0,), (0,)), ((), ())), preferred_element_type=jnp.float32
    )


def place():
    dp, ex = lax.axis_index("dp"), lax.axis_index("expert")
    return dp, ex, dp // (RING * CORES), (dp // CORES) % RING, dp % CORES


def index_of(z, y, core):
    return ((z % RING) * RING + y % RING) * CORES + core


def send(src, dst, send_sem, recv_sem, device):
    return pltpu.make_async_remote_copy(
        src_ref=src,
        dst_ref=dst,
        send_sem=send_sem,
        recv_sem=recv_sem,
        device_id=device,
        device_id_type=MESH,
    )


def greet(devices, experts, dp, ex):
    barrier = pltpu.get_barrier_semaphore()
    for device in devices:
        pl.semaphore_signal(barrier, inc=1, device_id=device, device_id_type=MESH)

    def one(step, carry):
        pl.semaphore_signal(
            barrier, inc=1, device_id=(dp, (ex + step) % experts), device_id_type=MESH
        )
        return carry

    lax.fori_loop(1, experts, one, 0)
    pl.semaphore_wait(barrier, len(devices) + experts - 1)


def exchange(experts, dp, ex, src, dst, send_sems, recv_sems):
    def copy(step):
        target = (ex + step) % experts
        return send(
            src.at[target], dst.at[ex], send_sems.at[target], recv_sems.at[ex], (dp, target)
        )

    def start(step, carry):
        copy(step).start()
        return carry

    def finish(step, carry):
        other = (ex + step) % experts
        send(
            src.at[other], dst.at[other], send_sems.at[other], recv_sems.at[other], (dp, other)
        ).wait()
        return carry

    lax.fori_loop(1, experts, start, 0)
    return lambda: lax.fori_loop(1, experts, finish, 0)


def dispatch_kernel(
    experts,
    weight_ref,
    in_ref,
    up_ref,
    whole_ref,
    recv_in_ref,
    recv_up_ref,
    local_sems,
    in_send,
    in_recv,
    up_send,
    up_recv,
    z_send,
    z_recv,
    y_send,
    y_recv,
    c_send,
    c_recv,
):
    dp, ex, z, y, core = place()
    half = weight_ref.shape[0] // 2
    right, left = (index_of(z + 1, y, core), ex), (index_of(z + 3, y, core), ex)
    sibling = (index_of(z, y, 1 - core), ex)
    ring_y = [(index_of(z, y + s, core), ex) for s in range(1, RING)]
    greet([right, left, sibling] + ring_y, experts, dp, ex)

    own = [
        pltpu.make_async_copy(weight_ref, whole_ref.at[dp], local_sems.at[0]),
        pltpu.make_async_copy(in_ref.at[ex], recv_in_ref.at[ex], local_sems.at[1]),
        pltpu.make_async_copy(up_ref.at[ex], recv_up_ref.at[ex], local_sems.at[2]),
    ]
    for copy in own:
        copy.start()

    sent = []

    def start(copy):
        copy.start()
        sent.append(copy)

    blocks = [dp, left[0], right[0], index_of(z + 2, y, core)]
    low, high = pl.ds(0, half), pl.ds(half, half)

    def z_copy(i, src, index, part, device):
        return send(src, whole_ref.at[index, part], z_send.at[i], z_recv.at[i], device)

    def z_arrival(i, index, part):
        there = whole_ref.at[index, part]
        return send(there, there, z_send.at[i], z_recv.at[i], right)

    whole = pl.ds(0, 2 * half)
    start(z_copy(0, weight_ref, dp, whole, right))
    start(z_copy(1, weight_ref, dp, whole, left))

    def spread(k, src):
        for s in range(1, RING):
            start(
                send(
                    src,
                    whole_ref.at[blocks[k]],
                    y_send.at[k, s - 1],
                    y_recv.at[k, s - 1],
                    ring_y[s - 1],
                )
            )
        start(send(src, whole_ref.at[blocks[k]], c_send.at[k, 0], c_recv.at[k, 0], sibling))

    def pass_on(k):
        for s in range(1, RING):
            index = index_of(blocks[k] // (RING * CORES), y + RING - s, core)
            there = whole_ref.at[index]
            send(there, there, y_send.at[k, s - 1], y_recv.at[k, s - 1], sibling).wait_recv()
            start(send(there, there, c_send.at[k, s], c_recv.at[k, s], sibling))

    spread(0, weight_ref)
    finish_in = exchange(experts, dp, ex, in_ref, recv_in_ref, in_send, in_recv)
    finish_up = exchange(experts, dp, ex, up_ref, recv_up_ref, up_send, up_recv)
    z_arrival(0, blocks[1], whole).wait_recv()
    start(z_copy(2, whole_ref.at[blocks[1], low], blocks[1], low, right))
    spread(1, whole_ref.at[blocks[1]])
    z_arrival(1, blocks[2], whole).wait_recv()
    start(z_copy(3, whole_ref.at[blocks[2], high], blocks[2], high, left))
    spread(2, whole_ref.at[blocks[2]])
    pass_on(0)
    z_arrival(2, blocks[3], low).wait_recv()
    z_arrival(3, blocks[3], high).wait_recv()
    spread(3, whole_ref.at[blocks[3]])
    pass_on(1)
    pass_on(2)
    pass_on(3)
    for k in range(RING):
        for s in range(RING):
            index = index_of(blocks[k] // (RING * CORES), y + RING - s, 1 - core)
            there = whole_ref.at[index]
            send(there, there, c_send.at[k, s], c_recv.at[k, s], sibling).wait_recv()
    for copy in sent:
        copy.wait_send()
    finish_in()
    finish_up()
    for copy in own:
        copy.wait()


def dispatch(weight, send_in, send_up, devices):
    experts = send_in.shape[0]
    dma = pltpu.SemaphoreType.DMA
    return pl.pallas_call(
        functools.partial(dispatch_kernel, experts),
        out_shape=[
            jax.ShapeDtypeStruct((devices,) + weight.shape, weight.dtype),
            jax.ShapeDtypeStruct(send_in.shape, send_in.dtype),
            jax.ShapeDtypeStruct(send_up.shape, send_up.dtype),
        ],
        in_specs=[ANY] * 3,
        out_specs=[ANY] * 3,
        scratch_shapes=[dma((3,))]
        + [dma((experts,))] * 4
        + [dma((RING,))] * 2
        + [dma((RING, RING - 1))] * 2
        + [dma((RING, RING))] * 2,
        compiler_params=pltpu.CompilerParams(collective_id=0, has_side_effects=True),
        name="dispatch",
    )(weight, send_in, send_up)


def middle(q, core):
    z = 2 + 2 * (q // RING)
    return (z + core * (7 - 2 * z)) * RING + q % RING


def middle_of(ex, core):
    z = ex // RING
    z = z + core * (7 - 2 * z)
    return (z % 2 == 0) & (z >= 2), (z // 2 - 1) * RING + ex % RING


def give_back_kernel(
    experts,
    out_ref,
    partial_ref,
    master_ref,
    first_ref,
    second_ref,
    source_ref,
    returned_ref,
    grads_ref,
    new_master_ref,
    new_first_ref,
    new_second_ref,
    c_buf,
    y_from,
    y_buf,
    z_from,
    z_buf,
    state,
    spread,
    ordered,
    arrived,
    local_sem,
    out_send,
    out_recv,
    c_send,
    c_recv,
    y_send,
    y_recv,
    z_send,
    z_recv,
    s_send,
    s_recv,
    t_send,
    t_recv,
):
    dp, ex, z, y, core = place()
    sibling = (index_of(z, y, 1 - core), ex)
    ring_y = [(index_of(z, y + s, core), ex) for s in range(1, RING)]
    ring_z = [(index_of(z + s, y, core), ex) for s in range(1, RING)]
    greet([sibling] + ring_y + ring_z, experts, dp, ex)

    to_core = send(partial_ref.at[:, :, 1 - core], c_buf, c_send, c_recv, sibling)
    to_core.start()
    own = pltpu.make_async_copy(out_ref.at[ex], returned_ref.at[ex], local_sem)
    own.start()
    finish_out = exchange(experts, dp, ex, out_ref, returned_ref, out_send, out_recv)
    to_core.wait()

    def pair(i, carry):
        at, row = i // RING, i % RING
        y_from[row, at] = (
            partial_ref[at, row, core].astype(jnp.float32) + c_buf[at, row].astype(jnp.float32)
        ).astype(y_from.dtype)
        return carry

    lax.fori_loop(0, RING * RING, pair, 0)
    y_copies = [
        send(
            y_from.at[(y + s) % RING],
            y_buf.at[s - 1],
            y_send.at[s - 1],
            y_recv.at[s - 1],
            ring_y[s - 1],
        )
        for s in range(1, RING)
    ]
    for copy in y_copies:
        copy.start()
    for copy in y_copies:
        copy.wait()

    def quad(i, carry):
        total = y_from[y, i].astype(jnp.float32)
        for s in range(RING - 1):
            total += y_buf[s, i].astype(jnp.float32)
        z_from[i] = total.astype(z_from.dtype)
        return carry

    lax.fori_loop(0, RING, quad, 0)
    z_copies = [
        send(
            z_from.at[(z + s) % RING],
            z_buf.at[s - 1],
            z_send.at[s - 1],
            z_recv.at[s - 1],
            ring_z[s - 1],
        )
        for s in range(1, RING)
    ]
    for copy in z_copies:
        copy.start()
    for copy in z_copies:
        copy.wait()
    grads = z_from[z].astype(jnp.float32)
    for s in range(RING - 1):
        grads += z_buf[s].astype(jnp.float32)
    grads_ref[...] = grads
    first = beta_first * first_ref[...] + (1.0 - beta_first) * grads
    second = beta_second * second_ref[...] + (1.0 - beta_second) * grads * grads
    updated = master_ref[...] - learn_rate * first / (jnp.sqrt(second) + adam_eps)
    tall, wide = state.shape[2:]
    pieces = state.shape[0]
    across = grads.shape[1] // wide

    def piece(q):
        return pl.ds(q // across * tall, tall), pl.ds(q % across * wide, wide)

    for i, value in enumerate((updated, first, second)):
        value = value.astype(state.dtype)
        for q in range(pieces):
            row, column = q // across * tall, q % across * wide
            state[q, i] = value[row : row + tall, column : column + wide]

    is_middle, mine = middle_of(ex, core)

    def spread_copy(q):
        return send(
            state.at[q], spread.at[ex], s_send.at[q], s_recv.at[ex], (dp, middle(q, core))
        )

    for q in range(pieces):

        @pl.when(middle(q, core) != ex)
        def _(q=q):
            spread_copy(q).start()

    def order_copy(step):
        target = (ex + step) % experts
        return send(
            ordered.at[target], arrived.at[mine], t_send.at[target], t_recv.at[mine], (dp, target)
        )

    @pl.when(is_middle)
    def _():
        spread[ex] = state[mine]

        def landed(step, carry):
            other = (ex + step) % experts
            there = spread.at[other]
            send(there, there, s_send.at[0], s_recv.at[other], (dp, other)).wait_recv()
            return carry

        def pick(e, carry):
            ordered[e] = spread[source_ref[e]]
            return carry

        def start(step, carry):
            order_copy(step).start()
            return carry

        lax.fori_loop(1, experts, landed, 0)
        lax.fori_loop(0, experts, pick, 0)
        lax.fori_loop(1, experts, start, 0)
        arrived[mine] = ordered[ex]

    for q in range(pieces):
        there = arrived.at[q]

        @pl.when(middle(q, core) != ex)
        def _(q=q, there=there):
            spread_copy(q).wait_send()
            send(
                there, there, t_send.at[0], t_recv.at[q], (dp, middle(q, core))
            ).wait_recv()

    for q in range(pieces):
        for i, ref in enumerate((new_master_ref, new_first_ref, new_second_ref)):
            ref[piece(q)] = arrived[q, i].astype(ref.dtype)

    @pl.when(is_middle)
    def _():
        def sent(step, carry):
            order_copy(step).wait_send()
            return carry

        lax.fori_loop(1, experts, sent, 0)

    finish_out()
    own.wait()


def give_back(outputs, partial, master, first_moment, second_moment, source):
    experts = outputs.shape[0]
    dma = pltpu.SemaphoreType.DMA
    block = partial.shape[3:]
    kind = partial.dtype
    piece = (3, 16, 128)
    pieces = block[0] * block[1] // (16 * 128)
    return pl.pallas_call(
        functools.partial(give_back_kernel, experts),
        out_shape=[jax.ShapeDtypeStruct(outputs.shape, outputs.dtype)]
        + [jax.ShapeDtypeStruct(block, jnp.float32)] * 4,
        in_specs=[ANY] + [VMEM] * 4 + [pl.BlockSpec(memory_space=pltpu.SMEM)],
        out_specs=[ANY] + [VMEM] * 4,
        scratch_shapes=[
            pltpu.VMEM((RING, RING) + block, kind),
            pltpu.VMEM((RING, RING) + block, kind),
            pltpu.VMEM((RING - 1, RING) + block, kind),
            pltpu.VMEM((RING,) + block, kind),
            pltpu.VMEM((RING - 1,) + block, kind),
            pltpu.VMEM((pieces,) + piece, kind),
            pltpu.VMEM((experts,) + piece, kind),
            pltpu.VMEM((experts,) + piece, kind),
            pltpu.VMEM((pieces,) + piece, kind),
            dma,
            dma((experts,)),
            dma((experts,)),
            dma,
            dma,
        ]
        + [dma((RING - 1,))] * 4
        + [dma((pieces,)), dma((experts,)), dma((experts,)), dma((pieces,))],
        compiler_params=pltpu.CompilerParams(
            collective_id=1, has_side_effects=True, vmem_limit_bytes=24 * 1024 * 1024
        ),
        name="give_back",
    )(outputs, partial, master, first_moment, second_moment, source)


def shards(
    tokens,
    route_ids,
    route_gates,
    cotangent,
    expert_weights,
    master,
    first_moment,
    second_moment,
    old_place,
    new_place,
):
    experts = lax.axis_size("expert")
    devices = lax.axis_size("dp")
    tok_rows, model = tokens.shape
    routes = route_ids.shape[1]
    capacity = 5 * tok_rows * routes // (4 * experts)
    slots = experts * capacity
    ff_width = expert_weights.shape[2] // 3
    expert_range = jnp.arange(experts, dtype=jnp.int32)
    holder = jnp.sum(
        expert_range[None, :] * (old_place[None, :] == expert_range[:, None]).astype(jnp.int32),
        axis=1,
    )
    flat_ids = route_ids.reshape(-1)
    onehot = (flat_ids[:, None] == expert_range[None, :]).astype(jnp.int32)
    rank_in = jnp.sum((jnp.cumsum(onehot, axis=0) - onehot) * onehot, axis=1)
    target = jnp.sum(onehot * holder[None, :], axis=1)
    slot_index = target * capacity + rank_in
    slot_range = jnp.arange(slots, dtype=jnp.int32)
    place_pairs = (slot_range[:, None] == slot_index[None, :]).astype(jnp.bfloat16)
    place_tokens = jnp.sum(place_pairs.reshape(slots, tok_rows, routes), axis=2)
    send_in = jnp.dot(place_tokens, tokens, preferred_element_type=jnp.float32).astype(jnp.bfloat16)
    scaled = (route_gates[:, :, None] * cotangent[:, None, :].astype(jnp.float32)).astype(
        jnp.bfloat16
    )
    send_up = jnp.dot(
        place_pairs, scaled.reshape(tok_rows * routes, -1), preferred_element_type=jnp.float32
    ).astype(jnp.bfloat16)
    packed = (experts, capacity * model // 128, 128)
    weight, recv_in, recv_up = dispatch(
        expert_weights[0], send_in.reshape(packed), send_up.reshape(packed), devices
    )
    weight = weight.reshape(model, -1)
    recv_in = recv_in.reshape(slots, model)
    recv_up = recv_up.reshape(slots, model)
    gate_val = jnp.dot(recv_in, weight[:, :ff_width], preferred_element_type=jnp.float32)
    up_val = jnp.dot(
        recv_in, weight[:, ff_width : 2 * ff_width], preferred_element_type=jnp.float32
    )
    hidden = (silu_value(gate_val) * up_val).astype(jnp.bfloat16)
    outputs = lax.dot_general(
        hidden,
        weight[:, 2 * ff_width :],
        (((1,), (1,)), ((), ())),
        preferred_element_type=jnp.float32,
    ).astype(jnp.bfloat16)
    partial = contract_rows(recv_up, hidden).astype(jnp.bfloat16)
    source_slot = jnp.sum(
        expert_range[None, :] * (old_place[None, :] == new_place[:, None]).astype(jnp.int32), axis=1
    )
    returned, *state = give_back(
        outputs.reshape(packed),
        partial.reshape(RING, RING, CORES, -1, ff_width),
        master[0],
        first_moment[0],
        second_moment[0],
        source_slot,
    )
    returned = returned.reshape(slots, model)
    picked = (
        jnp.take(returned, slot_index, axis=0).reshape(tok_rows, routes, -1).astype(jnp.float32)
    )
    combined = jnp.sum(route_gates[:, :, None] * picked, axis=1).astype(jnp.bfloat16)
    gate_grads = jnp.sum(cotangent[:, None, :].astype(jnp.float32) * picked, axis=2)
    return (combined, gate_grads) + tuple(value[None] for value in state)


def solution(mesh):
    in_specs = (
        P(("dp", "expert"), None),
        P(("dp", "expert"), None),
        P(("dp", "expert"), None),
        P(("dp", "expert"), None),
        P("expert", "dp", None),
        P("expert", "dp", None),
        P("expert", "dp", None),
        P("expert", "dp", None),
        P(),
        P(),
    )
    out_specs = (
        P(("dp", "expert"), None),
        P(("dp", "expert"), None),
        P("expert", "dp", None),
        P("expert", "dp", None),
        P("expert", "dp", None),
        P("expert", "dp", None),
    )
    return jax.shard_map(shards, mesh=mesh, in_specs=in_specs, out_specs=out_specs, check_vma=False)
```

```python
import functools

import jax
import jax.numpy as jnp
from jax import lax
from jax.experimental import pallas as pl
from jax.experimental.pallas import tpu as pltpu
from jax.sharding import PartitionSpec as P

beta_first = 0.9
beta_second = 0.999
learn_rate = 0.01
adam_eps = 1e-08

MESH = pl.DeviceIdType.MESH
VMEM = pl.BlockSpec(memory_space=pltpu.VMEM)
RING = 4
CORES = 2


def silu_value(values):
    return values * jax.nn.sigmoid(values)


def contract_rows(left, right):
    return lax.dot_general(
        left, right, (((0,), (0,)), ((), ())), preferred_element_type=jnp.float32
    )


def place():
    dp, ex = lax.axis_index("dp"), lax.axis_index("expert")
    return dp, ex, dp // (RING * CORES), (dp // CORES) % RING, dp % CORES


def index_of(z, y, core):
    return ((z % RING) * RING + y % RING) * CORES + core


def send(src, dst, send_sem, recv_sem, device):
    return pltpu.make_async_remote_copy(
        src_ref=src,
        dst_ref=dst,
        send_sem=send_sem,
        recv_sem=recv_sem,
        device_id=device,
        device_id_type=MESH,
    )


def greet(devices, experts, dp, ex):
    barrier = pltpu.get_barrier_semaphore()
    for device in devices:
        pl.semaphore_signal(barrier, inc=1, device_id=device, device_id_type=MESH)

    def one(step, carry):
        pl.semaphore_signal(
            barrier, inc=1, device_id=(dp, (ex + step) % experts), device_id_type=MESH
        )
        return carry

    lax.fori_loop(1, experts, one, 0)
    return lambda: pl.semaphore_wait(barrier, len(devices) + experts - 1)


def exchange(experts, dp, ex, src, dst, send_sems, recv_sems):
    def copy(step):
        target = (ex + step) % experts
        return send(
            src.at[target], dst.at[ex], send_sems.at[target], recv_sems.at[ex], (dp, target)
        )

    def start(step, carry):
        copy(step).start()
        return carry

    def arrival(step, carry):
        other = (ex + step) % experts
        there = dst.at[other]
        send(there, there, send_sems.at[other], recv_sems.at[other], (dp, other)).wait_recv()
        return carry

    def departure(step, carry):
        copy(step).wait_send()
        return carry

    lax.fori_loop(1, experts, start, 0)
    return (
        lambda: lax.fori_loop(1, experts, arrival, 0),
        lambda: lax.fori_loop(1, experts, departure, 0),
    )


def middle(q, core):
    z = 2 + 2 * (q // RING)
    return (z + core * (7 - 2 * z)) * RING + q % RING


def middle_of(ex, core):
    z = ex // RING
    z = z + core * (7 - 2 * z)
    return (z % 2 == 0) & (z >= 2), (z // 2 - 1) * RING + ex % RING


def layer_kernel(
    experts,
    place_ref,
    pick_ref,
    gates_ref,
    tokens_ref,
    cot_ref,
    weight_ref,
    master_ref,
    first_ref,
    second_ref,
    source_ref,
    combined_ref,
    gate_grads_ref,
    grads_ref,
    new_master_ref,
    new_first_ref,
    new_second_ref,
    whole,
    pack,
    rows,
    both,
    hidden,
    in_from,
    in_to,
    up_from,
    up_to,
    out_from,
    out_to,
    partial,
    c_buf,
    y_from,
    y_buf,
    z_from,
    z_buf,
    state,
    spread,
    ordered,
    arrived,
    local_sem,
    in_send,
    in_recv,
    up_send,
    up_recv,
    out_send,
    out_recv,
    wz_send,
    wz_recv,
    wy_send,
    wy_recv,
    wc_send,
    wc_recv,
    c_send,
    c_recv,
    y_send,
    y_recv,
    z_send,
    z_recv,
    s_send,
    s_recv,
    t_send,
    t_recv,
):
    dp, ex, z, y, core = place()
    sibling = (index_of(z, y, 1 - core), ex)
    ring_y = [(index_of(z, y + s, core), ex) for s in range(1, RING)]
    ring_z = [(index_of(z + s, y, core), ex) for s in range(1, RING)]
    right, left = ring_z[0], ring_z[2]
    all_here = greet([sibling] + ring_y + ring_z, experts, dp, ex)

    slots, model = rows.shape
    depth = weight_ref.shape[0]
    half = depth // 2
    ff = hidden.shape[1]
    lanes = pack.shape[1]
    per_row = model // lanes
    block = in_from.shape[1]
    wide_step = 2 * lanes
    steps = model // wide_step

    def columns(i, width):
        return pl.ds(pl.multiple_of(i * width, width), width)

    def pack_column(c, value):
        pack[pl.ds(c, slots, stride=per_row), :] = value

    def to_blocks(dst):
        def one(i, carry):
            dst[i] = pack[columns(i, block), :].astype(dst.dtype)
            return carry

        lax.fori_loop(0, experts, one, 0)

    def to_rows(src):
        def one(i, carry):
            pack[columns(i, block), :] = src[i].astype(jnp.float32)
            return carry

        def other(c, carry):
            rows[:, columns(c, lanes)] = pack[pl.ds(c, slots, stride=per_row), :].astype(rows.dtype)
            return carry

        lax.fori_loop(0, experts, one, 0)
        lax.fori_loop(0, per_row, other, 0)

    def place_in(c, carry):
        value = tokens_ref[:, columns(c, lanes)]
        pack_column(c, jnp.dot(place_ref[...], value, preferred_element_type=jnp.float32))
        return carry

    def place_up(c, carry):
        value = gates_ref[...] * cot_ref[:, columns(c, lanes)].astype(jnp.float32)
        value = value.astype(cot_ref.dtype)
        pack_column(c, jnp.dot(place_ref[...], value, preferred_element_type=jnp.float32))
        return carry

    lax.fori_loop(0, per_row, place_in, 0)
    to_blocks(in_from)
    all_here()

    sent = []

    def start(copy):
        copy.start()
        sent.append(copy)

    def slot(index, first=0, count=depth):
        return whole.at[pl.ds(pl.multiple_of(index * depth + first, half), count), :]

    blocks = [dp, left[0], right[0], ring_z[1][0]]

    def z_copy(i, src, index, part, device):
        return send(src, slot(index, *part), wz_send.at[i], wz_recv.at[i], device)

    def z_arrival(i, index, part):
        there = slot(index, *part)
        send(there, there, wz_send.at[i], wz_recv.at[i], right).wait_recv()

    every, low, high = (0, depth), (0, half), (half, half)

    def spread_weight(k, src):
        for s in range(1, RING):
            start(
                send(
                    src,
                    slot(blocks[k]),
                    wy_send.at[k, s - 1],
                    wy_recv.at[k, s - 1],
                    ring_y[s - 1],
                )
            )
        start(send(src, slot(blocks[k]), wc_send.at[k, 0], wc_recv.at[k, 0], sibling))

    def pass_on(k):
        for s in range(1, RING):
            there = slot(index_of(blocks[k] // (RING * CORES), y + RING - s, core))
            send(there, there, wy_send.at[k, s - 1], wy_recv.at[k, s - 1], sibling).wait_recv()
            start(send(there, there, wc_send.at[k, s], wc_recv.at[k, s], sibling))

    own = pltpu.make_async_copy(weight_ref, slot(dp), local_sem)
    own.start()
    start(z_copy(0, weight_ref, dp, every, right))
    start(z_copy(1, weight_ref, dp, every, left))
    in_there, in_left = exchange(experts, dp, ex, in_from, in_to, in_send, in_recv)
    spread_weight(0, weight_ref)
    in_to[ex] = in_from[ex]
    lax.fori_loop(0, per_row, place_up, 0)
    to_blocks(up_from)
    up_there, up_left = exchange(experts, dp, ex, up_from, up_to, up_send, up_recv)
    up_to[ex] = up_from[ex]
    z_arrival(0, blocks[1], every)
    start(z_copy(2, slot(blocks[1], *low), blocks[1], low, right))
    spread_weight(1, slot(blocks[1]))
    z_arrival(1, blocks[2], every)
    start(z_copy(3, slot(blocks[2], *high), blocks[2], high, left))
    spread_weight(2, slot(blocks[2]))
    pass_on(0)
    z_arrival(2, blocks[3], low)
    z_arrival(3, blocks[3], high)
    spread_weight(3, slot(blocks[3]))
    in_there()
    to_rows(in_to)
    pass_on(1)
    pass_on(2)
    pass_on(3)
    for k in range(RING):
        for s in range(RING):
            there = slot(index_of(blocks[k] // (RING * CORES), y + RING - s, 1 - core))
            send(there, there, wc_send.at[k, s], wc_recv.at[k, s], sibling).wait_recv()
    own.wait()

    both[...] = jnp.zeros_like(both)

    def gate_up(i, carry):
        both[...] += jnp.dot(
            rows[:, columns(i, wide_step)],
            whole[columns(i, wide_step), pl.ds(0, 2 * ff)],
            preferred_element_type=jnp.float32,
        )
        return carry

    lax.fori_loop(0, steps, gate_up, 0)
    hidden[...] = (silu_value(both[:, :ff]) * both[:, ff:]).astype(hidden.dtype)

    def down(i, carry):
        value = lax.dot_general(
            hidden[...],
            whole[columns(i, wide_step), pl.ds(2 * ff, ff)],
            (((1,), (1,)), ((), ())),
            preferred_element_type=jnp.float32,
        )
        pack_column(2 * i, value[:, :lanes])
        pack_column(2 * i + 1, value[:, lanes:])
        return carry

    lax.fori_loop(0, steps, down, 0)
    to_blocks(out_from)
    out_there, out_left = exchange(experts, dp, ex, out_from, out_to, out_send, out_recv)
    out_to[ex] = out_from[ex]

    up_there()
    to_rows(up_to)
    pairs = wide_step // (CORES * depth)

    def grad(i, carry):
        value = contract_rows(rows[:, columns(i, wide_step)], hidden[...]).astype(partial.dtype)
        partial[pl.ds(i * pairs, pairs)] = value.reshape((pairs, CORES, depth, ff))
        return carry

    lax.fori_loop(0, steps, grad, 0)
    to_core = send(partial.at[:, 1 - core], c_buf, c_send, c_recv, sibling)
    to_core.start()
    to_core.wait()

    def pair(i, carry):
        at, row = i // RING, i % RING
        y_from[row, at] = (
            partial[i, core].astype(jnp.float32) + c_buf[i].astype(jnp.float32)
        ).astype(y_from.dtype)
        return carry

    lax.fori_loop(0, RING * RING, pair, 0)
    y_copies = [
        send(
            y_from.at[(y + s) % RING],
            y_buf.at[s - 1],
            y_send.at[s - 1],
            y_recv.at[s - 1],
            ring_y[s - 1],
        )
        for s in range(1, RING)
    ]
    for copy in y_copies:
        copy.start()
    for copy in y_copies:
        copy.wait()

    def quad(i, carry):
        total = y_from[y, i].astype(jnp.float32)
        for s in range(RING - 1):
            total += y_buf[s, i].astype(jnp.float32)
        z_from[i] = total.astype(z_from.dtype)
        return carry

    lax.fori_loop(0, RING, quad, 0)
    z_copies = [
        send(
            z_from.at[(z + s) % RING],
            z_buf.at[s - 1],
            z_send.at[s - 1],
            z_recv.at[s - 1],
            ring_z[s - 1],
        )
        for s in range(1, RING)
    ]
    for copy in z_copies:
        copy.start()
    for copy in z_copies:
        copy.wait()
    grads = z_from[z].astype(jnp.float32)
    for s in range(RING - 1):
        grads += z_buf[s].astype(jnp.float32)
    grads_ref[...] = grads
    first = beta_first * first_ref[...] + (1.0 - beta_first) * grads
    second = beta_second * second_ref[...] + (1.0 - beta_second) * grads * grads
    updated = master_ref[...] - learn_rate * first / (jnp.sqrt(second) + adam_eps)
    tall, wide = state.shape[2:]
    pieces = state.shape[0]
    across = grads.shape[1] // wide

    def piece(q):
        return pl.ds(q // across * tall, tall), pl.ds(q % across * wide, wide)

    for i, value in enumerate((updated, first, second)):
        value = value.astype(state.dtype)
        for q in range(pieces):
            row, column = q // across * tall, q % across * wide
            state[q, i] = value[row : row + tall, column : column + wide]

    is_middle, mine = middle_of(ex, core)

    def spread_copy(q):
        return send(
            state.at[q], spread.at[ex], s_send.at[q], s_recv.at[ex], (dp, middle(q, core))
        )

    for q in range(pieces):

        @pl.when(middle(q, core) != ex)
        def _(q=q):
            spread_copy(q).start()

    def order_copy(step):
        target = (ex + step) % experts
        return send(
            ordered.at[target], arrived.at[mine], t_send.at[target], t_recv.at[mine], (dp, target)
        )

    @pl.when(is_middle)
    def _():
        spread[ex] = state[mine]

        def landed(step, carry):
            other = (ex + step) % experts
            there = spread.at[other]
            send(there, there, s_send.at[0], s_recv.at[other], (dp, other)).wait_recv()
            return carry

        def pick(e, carry):
            ordered[e] = spread[source_ref[e]]
            return carry

        def start(step, carry):
            order_copy(step).start()
            return carry

        lax.fori_loop(1, experts, landed, 0)
        lax.fori_loop(0, experts, pick, 0)
        lax.fori_loop(1, experts, start, 0)
        arrived[mine] = ordered[ex]

    for q in range(pieces):
        there = arrived.at[q]

        @pl.when(middle(q, core) != ex)
        def _(q=q, there=there):
            spread_copy(q).wait_send()
            send(
                there, there, t_send.at[0], t_recv.at[q], (dp, middle(q, core))
            ).wait_recv()

    for q in range(pieces):
        for i, ref in enumerate((new_master_ref, new_first_ref, new_second_ref)):
            ref[piece(q)] = arrived[q, i].astype(ref.dtype)

    @pl.when(is_middle)
    def _():
        def sent(step, carry):
            order_copy(step).wait_send()
            return carry

        lax.fori_loop(1, experts, sent, 0)

    out_there()
    to_rows(out_to)

    def combine(c, total):
        value = jnp.dot(
            pick_ref[...], rows[:, columns(c, lanes)], preferred_element_type=jnp.float32
        )
        combined_ref[:, columns(c, lanes)] = (gates_ref[...] * value).astype(combined_ref.dtype)
        return total + cot_ref[:, columns(c, lanes)].astype(jnp.float32) * value

    total = lax.fori_loop(
        0, per_row, combine, jnp.zeros((tokens_ref.shape[0], lanes), jnp.float32)
    )
    gate_grads_ref[...] = jnp.sum(total, axis=1, keepdims=True)
    for copy in sent:
        copy.wait_send()
    in_left()
    up_left()
    out_left()


def layer(place_slots, gates, tokens, cotangent, weight, state, source):
    slots, tok_rows = place_slots.shape
    model = tokens.shape[1]
    experts = source.shape[0]
    depth, ff = weight.shape[0], weight.shape[1] // 3
    dma = pltpu.SemaphoreType.DMA
    kind = tokens.dtype
    lanes = 128
    packed = (experts, slots * model // lanes // experts, lanes)
    block = (depth, ff)
    piece = (3, 16, 128)
    pieces = depth * ff // (16 * 128)

    def sixteen(*shape):
        return pltpu.VMEM(shape, kind)

    return pl.pallas_call(
        functools.partial(layer_kernel, experts),
        out_shape=[
            jax.ShapeDtypeStruct(tokens.shape, kind),
            jax.ShapeDtypeStruct((tok_rows, 1), jnp.float32),
        ]
        + [jax.ShapeDtypeStruct(block, jnp.float32)] * 4,
        in_specs=[VMEM] * 9 + [pl.BlockSpec(memory_space=pltpu.SMEM)],
        out_specs=[VMEM] * 6,
        scratch_shapes=[
            sixteen(model, 3 * ff),
            pltpu.VMEM((slots * model // lanes, lanes), jnp.float32),
            sixteen(slots, model),
            pltpu.VMEM((slots, 2 * ff), jnp.float32),
            sixteen(slots, ff),
        ]
        + [sixteen(*packed)] * 6
        + [
            sixteen(RING * RING, CORES, *block),
            sixteen(RING * RING, *block),
            sixteen(RING, RING, *block),
            sixteen(RING - 1, RING, *block),
            sixteen(RING, *block),
            sixteen(RING - 1, *block),
            sixteen(pieces, *piece),
            sixteen(experts, *piece),
            sixteen(experts, *piece),
            sixteen(pieces, *piece),
            dma,
        ]
        + [dma((experts,))] * 6
        + [dma((RING,))] * 2
        + [dma((RING, RING - 1))] * 2
        + [dma((RING, RING))] * 2
        + [dma] * 2
        + [dma((RING - 1,))] * 4
        + [dma((pieces,)), dma((experts,)), dma((experts,)), dma((pieces,))],
        compiler_params=pltpu.CompilerParams(
            collective_id=0, has_side_effects=True, vmem_limit_bytes=40 * 1024 * 1024
        ),
        name="layer",
    )(place_slots, place_slots.T, gates, tokens, cotangent, weight, *state, source)


def shards(
    tokens,
    route_ids,
    route_gates,
    cotangent,
    expert_weights,
    master,
    first_moment,
    second_moment,
    old_place,
    new_place,
):
    experts = lax.axis_size("expert")
    tok_rows = tokens.shape[0]
    routes = route_ids.shape[1]
    capacity = 5 * tok_rows * routes // (4 * experts)
    slots = experts * capacity
    expert_range = jnp.arange(experts, dtype=jnp.int32)
    holder = jnp.sum(
        expert_range[None, :] * (old_place[None, :] == expert_range[:, None]).astype(jnp.int32),
        axis=1,
    )
    flat_ids = route_ids.reshape(-1)
    onehot = (flat_ids[:, None] == expert_range[None, :]).astype(jnp.int32)
    rank_in = jnp.sum((jnp.cumsum(onehot, axis=0) - onehot) * onehot, axis=1)
    target = jnp.sum(onehot * holder[None, :], axis=1)
    slot_index = target * capacity + rank_in
    slot_range = jnp.arange(slots, dtype=jnp.int32)
    place_pairs = (slot_range[:, None] == slot_index[None, :]).astype(jnp.bfloat16)
    source_slot = jnp.sum(
        expert_range[None, :] * (old_place[None, :] == new_place[:, None]).astype(jnp.int32), axis=1
    )
    combined, gate_grads, *state = layer(
        place_pairs,
        route_gates,
        tokens,
        cotangent,
        expert_weights[0],
        (master[0], first_moment[0], second_moment[0]),
        source_slot,
    )
    return (combined, gate_grads) + tuple(value[None] for value in state)


def solution(mesh):
    in_specs = (
        P(("dp", "expert"), None),
        P(("dp", "expert"), None),
        P(("dp", "expert"), None),
        P(("dp", "expert"), None),
        P("expert", "dp", None),
        P("expert", "dp", None),
        P("expert", "dp", None),
        P("expert", "dp", None),
        P(),
        P(),
    )
    out_specs = (
        P(("dp", "expert"), None),
        P(("dp", "expert"), None),
        P("expert", "dp", None),
        P("expert", "dp", None),
        P("expert", "dp", None),
        P("expert", "dp", None),
    )
    return jax.shard_map(shards, mesh=mesh, in_specs=in_specs, out_specs=out_specs, check_vma=False)
```

```python
import functools

import jax
import jax.numpy as jnp
from jax import lax
from jax.experimental import pallas as pl
from jax.experimental.pallas import tpu as pltpu
from jax.sharding import PartitionSpec as P

beta_first = 0.9
beta_second = 0.999
learn_rate = 0.01
adam_eps = 1e-08

MESH = pl.DeviceIdType.MESH
VMEM = pl.BlockSpec(memory_space=pltpu.VMEM)
RING = 4
CORES = 2


def silu_value(values):
    return values * jax.nn.sigmoid(values)


def contract_rows(left, right):
    return lax.dot_general(
        left, right, (((0,), (0,)), ((), ())), preferred_element_type=jnp.float32
    )


def place():
    dp, ex = lax.axis_index("dp"), lax.axis_index("expert")
    return dp, ex, dp // (RING * CORES), (dp // CORES) % RING, dp % CORES


def index_of(z, y, core):
    return ((z % RING) * RING + y % RING) * CORES + core


def send(src, dst, send_sem, recv_sem, device):
    return pltpu.make_async_remote_copy(
        src_ref=src,
        dst_ref=dst,
        send_sem=send_sem,
        recv_sem=recv_sem,
        device_id=device,
        device_id_type=MESH,
    )


def greet(devices, experts, dp, ex):
    barrier = pltpu.get_barrier_semaphore()
    for device in devices:
        pl.semaphore_signal(barrier, inc=1, device_id=device, device_id_type=MESH)

    def one(step, carry):
        pl.semaphore_signal(
            barrier, inc=1, device_id=(dp, (ex + step) % experts), device_id_type=MESH
        )
        return carry

    lax.fori_loop(1, experts, one, 0)
    return lambda: pl.semaphore_wait(barrier, len(devices) + experts - 1)


def exchange(experts, dp, ex, src, dst, send_sems, recv_sems):
    def copy(step):
        target = (ex + step) % experts
        return send(
            src.at[target], dst.at[ex], send_sems.at[target], recv_sems.at[ex], (dp, target)
        )

    def start(step, carry):
        copy(step).start()
        return carry

    def arrival(step, carry):
        other = (ex + step) % experts
        there = dst.at[other]
        send(there, there, send_sems.at[other], recv_sems.at[other], (dp, other)).wait_recv()
        return carry

    def departure(step, carry):
        copy(step).wait_send()
        return carry

    lax.fori_loop(1, experts, start, 0)
    return (
        lambda: lax.fori_loop(1, experts, arrival, 0),
        lambda: lax.fori_loop(1, experts, departure, 0),
    )


def middle(q, core):
    z = 2 + 2 * (q // RING)
    return (z + core * (7 - 2 * z)) * RING + q % RING


def middle_of(ex, core):
    z = ex // RING
    z = z + core * (7 - 2 * z)
    return (z % 2 == 0) & (z >= 2), (z // 2 - 1) * RING + ex % RING


def layer_kernel(
    experts,
    place_ref,
    pick_ref,
    gates_ref,
    tokens_ref,
    cot_ref,
    weight_ref,
    master_ref,
    first_ref,
    second_ref,
    source_ref,
    combined_ref,
    gate_grads_ref,
    grads_ref,
    new_master_ref,
    new_first_ref,
    new_second_ref,
    whole,
    whole_down,
    pack,
    rows,
    rows_up,
    both,
    hidden,
    in_from,
    in_to,
    up_from,
    up_to,
    out_from,
    out_to,
    partial,
    c_buf,
    y_from,
    y_buf,
    z_from,
    z_buf,
    state,
    spread,
    ordered,
    arrived,
    local_sem,
    in_send,
    in_recv,
    up_send,
    up_recv,
    out_send,
    out_recv,
    wz_send,
    wz_recv,
    wy_send,
    wy_recv,
    wc_send,
    wc_recv,
    dz_send,
    dz_recv,
    dy_send,
    dy_recv,
    dc_send,
    dc_recv,
    c_send,
    c_recv,
    y_send,
    y_recv,
    z_send,
    z_recv,
    s_send,
    s_recv,
    t_send,
    t_recv,
):
    dp, ex, z, y, core = place()
    sibling = (index_of(z, y, 1 - core), ex)
    ring_y = [(index_of(z, y + s, core), ex) for s in range(1, RING)]
    ring_z = [(index_of(z + s, y, core), ex) for s in range(1, RING)]
    right, left = ring_z[0], ring_z[2]
    all_here = greet([sibling] + ring_y + ring_z, experts, dp, ex)

    slots, model = rows.shape
    depth = weight_ref.shape[0]
    ff = hidden.shape[1]
    lanes = pack.shape[1]
    per_row = model // lanes
    block = in_from.shape[1]
    quarter = model // RING
    group = per_row // RING

    def columns(i, width):
        return pl.ds(pl.multiple_of(i * width, width), width)

    def pack_columns(i, value):
        for c in range(group):
            pack[pl.ds(i * group + c, slots, stride=per_row), :] = value[
                :, c * lanes : (c + 1) * lanes
            ]

    def to_blocks(dst):
        several = experts // RING

        def one(i, carry):
            value = pack[columns(i, several * block), :].astype(dst.dtype)
            dst[pl.ds(i * several, several)] = value.reshape((several, block, lanes))
            return carry

        lax.fori_loop(0, RING, one, 0)

    def to_rows(src, dst):
        several = experts // RING

        def one(i, carry):
            value = src[pl.ds(i * several, several)].astype(jnp.float32)
            pack[columns(i, several * block), :] = value.reshape((several * block, lanes))
            return carry

        def other(i, carry):
            for c in range(group):
                value = pack[pl.ds(i * group + c, slots, stride=per_row), :]
                dst[:, columns(i * group + c, lanes)] = value.astype(dst.dtype)
            return carry

        lax.fori_loop(0, RING, one, 0)
        lax.fori_loop(0, RING, other, 0)

    def place_in(i, carry):
        value = tokens_ref[:, columns(i, quarter)]
        pack_columns(i, jnp.dot(place_ref[...], value, preferred_element_type=jnp.float32))
        return carry

    def place_up(i, carry):
        value = gates_ref[...] * cot_ref[:, columns(i, quarter)].astype(jnp.float32)
        value = value.astype(cot_ref.dtype)
        pack_columns(i, jnp.dot(place_ref[...], value, preferred_element_type=jnp.float32))
        return carry

    lax.fori_loop(0, RING, place_in, 0)
    to_blocks(in_from)
    all_here()

    sent = []

    def start(copy):
        copy.start()
        sent.append(copy)

    blocks = [dp, left[0], right[0], ring_z[1][0]]
    half = depth // 2
    every, low, high = (0, depth), (0, half), (half, half)

    def gather(src, dst, zs, zr, ys, yr, cs, cr):
        def slot(index, first=0, count=depth):
            return dst.at[pl.ds(pl.multiple_of(index * depth + first, half), count), :]

        def z_copy(i, from_ref, index, part, device):
            return send(from_ref, slot(index, *part), zs.at[i], zr.at[i], device)

        def z_arrival(i, index, part):
            there = slot(index, *part)
            send(there, there, zs.at[i], zr.at[i], right).wait_recv()

        def spread_weight(k, from_ref):
            for s in range(1, RING):
                start(
                    send(
                        from_ref,
                        slot(blocks[k]),
                        ys.at[k, s - 1],
                        yr.at[k, s - 1],
                        ring_y[s - 1],
                    )
                )
            start(send(from_ref, slot(blocks[k]), cs.at[k, 0], cr.at[k, 0], sibling))

        def begin():
            start(z_copy(0, src, dp, every, right))
            start(z_copy(1, src, dp, every, left))
            spread_weight(0, src)

        def neighbours():
            z_arrival(0, blocks[1], every)
            start(z_copy(2, slot(blocks[1], *low), blocks[1], low, right))
            spread_weight(1, slot(blocks[1]))
            z_arrival(1, blocks[2], every)
            start(z_copy(3, slot(blocks[2], *high), blocks[2], high, left))
            spread_weight(2, slot(blocks[2]))

        def opposite():
            z_arrival(2, blocks[3], low)
            z_arrival(3, blocks[3], high)
            spread_weight(3, slot(blocks[3]))

        def pass_on(k):
            for s in range(1, RING):
                there = slot(index_of(blocks[k] // (RING * CORES), y + RING - s, core))
                send(there, there, ys.at[k, s - 1], yr.at[k, s - 1], sibling).wait_recv()
                start(send(there, there, cs.at[k, s], cr.at[k, s], sibling))

        def complete(k):
            for s in range(RING):
                there = slot(index_of(blocks[k] // (RING * CORES), y + RING - s, 1 - core))
                send(there, there, cs.at[k, s], cr.at[k, s], sibling).wait_recv()

        own = pltpu.make_async_copy(src, slot(dp), local_sem.at[0 if dst is whole else 1])
        return own, begin, neighbours, opposite, pass_on, complete

    gate_up = gather(
        weight_ref.at[:, pl.ds(0, 2 * ff)],
        whole,
        wz_send,
        wz_recv,
        wy_send,
        wy_recv,
        wc_send,
        wc_recv,
    )
    down = gather(
        weight_ref.at[:, pl.ds(2 * ff, ff)],
        whole_down,
        dz_send,
        dz_recv,
        dy_send,
        dy_recv,
        dc_send,
        dc_recv,
    )
    own, begin, neighbours, opposite, pass_on, complete = gate_up
    begin()
    in_there, in_left = exchange(experts, dp, ex, in_from, in_to, in_send, in_recv)
    own.start()
    in_to[ex] = in_from[ex]
    lax.fori_loop(0, RING, place_up, 0)
    to_blocks(up_from)
    up_there, up_left = exchange(experts, dp, ex, up_from, up_to, up_send, up_recv)
    up_to[ex] = up_from[ex]
    both[...] = jnp.zeros_like(both)
    neighbours()
    pass_on(0)
    in_there()
    to_rows(in_to, rows)
    own.wait()

    def multiply(k):
        complete(k)
        part = columns(blocks[k] // (RING * CORES), quarter)
        both[...] += jnp.dot(rows[:, part], whole[part, :], preferred_element_type=jnp.float32)

    opposite()
    pass_on(1)
    pass_on(2)
    multiply(0)
    multiply(1)
    multiply(2)
    pass_on(3)
    up_there()
    to_rows(up_to, rows_up)
    multiply(3)
    own, begin, neighbours, opposite, pass_on, complete = down
    begin()
    own.start()
    hidden[...] = (silu_value(both[:, :ff]) * both[:, ff:]).astype(hidden.dtype)

    def grad(i, carry):
        value = contract_rows(rows_up[:, columns(i, quarter)], hidden[...]).astype(partial.dtype)
        partial[pl.ds(i * RING, RING)] = value.reshape((RING, CORES, depth, ff))
        return carry

    lax.fori_loop(0, RING, grad, 0)
    to_core = send(partial.at[:, 1 - core], c_buf, c_send, c_recv, sibling)
    to_core.start()
    to_core.wait()

    def pair(i, carry):
        at, row = i // RING, i % RING
        y_from[row, at] = (
            partial[i, core].astype(jnp.float32) + c_buf[i].astype(jnp.float32)
        ).astype(y_from.dtype)
        return carry

    lax.fori_loop(0, RING * RING, pair, 0)
    y_copies = [
        send(
            y_from.at[(y + s) % RING],
            y_buf.at[s - 1],
            y_send.at[s - 1],
            y_recv.at[s - 1],
            ring_y[s - 1],
        )
        for s in range(1, RING)
    ]
    for copy in y_copies:
        copy.start()
    neighbours()
    pass_on(0)
    for copy in y_copies:
        copy.wait()

    def quad(i, carry):
        total = y_from[y, i].astype(jnp.float32)
        for s in range(RING - 1):
            total += y_buf[s, i].astype(jnp.float32)
        z_from[i] = total.astype(z_from.dtype)
        return carry

    lax.fori_loop(0, RING, quad, 0)
    z_copies = [
        send(
            z_from.at[(z + s) % RING],
            z_buf.at[s - 1],
            z_send.at[s - 1],
            z_recv.at[s - 1],
            ring_z[s - 1],
        )
        for s in range(1, RING)
    ]
    for copy in z_copies:
        copy.start()
    opposite()
    for k in range(1, RING):
        pass_on(k)
    for k in range(RING):
        complete(k)
    own.wait()

    def outputs(i, carry):
        value = lax.dot_general(
            hidden[...],
            whole_down[columns(i, quarter), :],
            (((1,), (1,)), ((), ())),
            preferred_element_type=jnp.float32,
        )
        pack_columns(i, value)
        return carry

    lax.fori_loop(0, RING, outputs, 0)
    to_blocks(out_from)
    out_there, out_left = exchange(experts, dp, ex, out_from, out_to, out_send, out_recv)
    out_to[ex] = out_from[ex]
    for copy in z_copies:
        copy.wait()
    grads = z_from[z].astype(jnp.float32)
    for s in range(RING - 1):
        grads += z_buf[s].astype(jnp.float32)
    grads_ref[...] = grads
    first = beta_first * first_ref[...] + (1.0 - beta_first) * grads
    second = beta_second * second_ref[...] + (1.0 - beta_second) * grads * grads
    updated = master_ref[...] - learn_rate * first / (jnp.sqrt(second) + adam_eps)
    tall, wide = state.shape[2:]
    pieces = state.shape[0]
    across = grads.shape[1] // wide

    def piece(q):
        return pl.ds(q // across * tall, tall), pl.ds(q % across * wide, wide)

    for i, value in enumerate((updated, first, second)):
        value = value.astype(state.dtype)
        for q in range(pieces):
            row, column = q // across * tall, q % across * wide
            state[q, i] = value[row : row + tall, column : column + wide]

    is_middle, mine = middle_of(ex, core)

    def spread_copy(q):
        return send(
            state.at[q], spread.at[ex], s_send.at[q], s_recv.at[ex], (dp, middle(q, core))
        )

    for q in range(pieces):

        @pl.when(middle(q, core) != ex)
        def _(q=q):
            spread_copy(q).start()

    def order_copy(step):
        target = (ex + step) % experts
        return send(
            ordered.at[target], arrived.at[mine], t_send.at[target], t_recv.at[mine], (dp, target)
        )

    @pl.when(is_middle)
    def _():
        spread[ex] = state[mine]

        def landed(step, carry):
            other = (ex + step) % experts
            there = spread.at[other]
            send(there, there, s_send.at[0], s_recv.at[other], (dp, other)).wait_recv()
            return carry

        def pick(e, carry):
            ordered[e] = spread[source_ref[e]]
            return carry

        def start(step, carry):
            order_copy(step).start()
            return carry

        lax.fori_loop(1, experts, landed, 0)
        lax.fori_loop(0, experts, pick, 0)
        lax.fori_loop(1, experts, start, 0)
        arrived[mine] = ordered[ex]

    out_there()
    to_rows(out_to, rows)

    def combine(i, total):
        part = columns(i, quarter)
        value = jnp.dot(pick_ref[...], rows[:, part], preferred_element_type=jnp.float32)
        combined_ref[:, part] = (gates_ref[...] * value).astype(combined_ref.dtype)
        return total + cot_ref[:, part].astype(jnp.float32) * value

    total = lax.fori_loop(
        0, RING, combine, jnp.zeros((tokens_ref.shape[0], quarter), jnp.float32)
    )
    gate_grads_ref[...] = jnp.sum(total, axis=1, keepdims=True)

    for q in range(pieces):
        there = arrived.at[q]

        @pl.when(middle(q, core) != ex)
        def _(q=q, there=there):
            spread_copy(q).wait_send()
            send(
                there, there, t_send.at[0], t_recv.at[q], (dp, middle(q, core))
            ).wait_recv()

    for q in range(pieces):
        for i, ref in enumerate((new_master_ref, new_first_ref, new_second_ref)):
            ref[piece(q)] = arrived[q, i].astype(ref.dtype)

    @pl.when(is_middle)
    def _():
        def sent(step, carry):
            order_copy(step).wait_send()
            return carry

        lax.fori_loop(1, experts, sent, 0)

    for copy in sent:
        copy.wait_send()
    in_left()
    up_left()
    out_left()


def layer(place_slots, gates, tokens, cotangent, weight, state, source):
    slots, tok_rows = place_slots.shape
    model = tokens.shape[1]
    experts = source.shape[0]
    depth, ff = weight.shape[0], weight.shape[1] // 3
    dma = pltpu.SemaphoreType.DMA
    kind = tokens.dtype
    lanes = 128
    packed = (experts, slots * model // lanes // experts, lanes)
    block = (depth, ff)
    piece = (3, 16, 128)
    pieces = depth * ff // (16 * 128)

    def sixteen(*shape):
        return pltpu.VMEM(shape, kind)

    return pl.pallas_call(
        functools.partial(layer_kernel, experts),
        out_shape=[
            jax.ShapeDtypeStruct(tokens.shape, kind),
            jax.ShapeDtypeStruct((tok_rows, 1), jnp.float32),
        ]
        + [jax.ShapeDtypeStruct(block, jnp.float32)] * 4,
        in_specs=[VMEM] * 9 + [pl.BlockSpec(memory_space=pltpu.SMEM)],
        out_specs=[VMEM] * 6,
        scratch_shapes=[
            sixteen(model, 2 * ff),
            sixteen(model, ff),
            pltpu.VMEM((slots * model // lanes, lanes), jnp.float32),
            sixteen(slots, model),
            sixteen(slots, model),
            pltpu.VMEM((slots, 2 * ff), jnp.float32),
            sixteen(slots, ff),
        ]
        + [sixteen(*packed)] * 6
        + [
            sixteen(RING * RING, CORES, *block),
            sixteen(RING * RING, *block),
            sixteen(RING, RING, *block),
            sixteen(RING - 1, RING, *block),
            sixteen(RING, *block),
            sixteen(RING - 1, *block),
            sixteen(pieces, *piece),
            sixteen(experts, *piece),
            sixteen(experts, *piece),
            sixteen(pieces, *piece),
            dma((2,)),
        ]
        + [dma((experts,))] * 6
        + ([dma((RING,))] * 2 + [dma((RING, RING - 1))] * 2 + [dma((RING, RING))] * 2) * 2
        + [dma] * 2
        + [dma((RING - 1,))] * 4
        + [dma((pieces,)), dma((experts,)), dma((experts,)), dma((pieces,))],
        compiler_params=pltpu.CompilerParams(
            collective_id=0, has_side_effects=True, vmem_limit_bytes=40 * 1024 * 1024
        ),
        name="layer",
    )(place_slots, place_slots.T, gates, tokens, cotangent, weight, *state, source)


def shards(
    tokens,
    route_ids,
    route_gates,
    cotangent,
    expert_weights,
    master,
    first_moment,
    second_moment,
    old_place,
    new_place,
):
    experts = lax.axis_size("expert")
    tok_rows = tokens.shape[0]
    routes = route_ids.shape[1]
    capacity = 5 * tok_rows * routes // (4 * experts)
    slots = experts * capacity
    expert_range = jnp.arange(experts, dtype=jnp.int32)
    holder = jnp.sum(
        expert_range[None, :] * (old_place[None, :] == expert_range[:, None]).astype(jnp.int32),
        axis=1,
    )
    flat_ids = route_ids.reshape(-1)
    onehot = (flat_ids[:, None] == expert_range[None, :]).astype(jnp.int32)
    rank_in = jnp.sum((jnp.cumsum(onehot, axis=0) - onehot) * onehot, axis=1)
    target = jnp.sum(onehot * holder[None, :], axis=1)
    slot_index = target * capacity + rank_in
    slot_range = jnp.arange(slots, dtype=jnp.int32)
    place_pairs = (slot_range[:, None] == slot_index[None, :]).astype(jnp.bfloat16)
    source_slot = jnp.sum(
        expert_range[None, :] * (old_place[None, :] == new_place[:, None]).astype(jnp.int32), axis=1
    )
    combined, gate_grads, *state = layer(
        place_pairs,
        route_gates,
        tokens,
        cotangent,
        expert_weights[0],
        (master[0], first_moment[0], second_moment[0]),
        source_slot,
    )
    return (combined, gate_grads) + tuple(value[None] for value in state)


def solution(mesh):
    in_specs = (
        P(("dp", "expert"), None),
        P(("dp", "expert"), None),
        P(("dp", "expert"), None),
        P(("dp", "expert"), None),
        P("expert", "dp", None),
        P("expert", "dp", None),
        P("expert", "dp", None),
        P("expert", "dp", None),
        P(),
        P(),
    )
    out_specs = (
        P(("dp", "expert"), None),
        P(("dp", "expert"), None),
        P("expert", "dp", None),
        P("expert", "dp", None),
        P("expert", "dp", None),
        P("expert", "dp", None),
    )
    return jax.shard_map(shards, mesh=mesh, in_specs=in_specs, out_specs=out_specs, check_vma=False)
```

```python
import functools

import jax
import jax.numpy as jnp
from jax import lax
from jax.experimental import pallas as pl
from jax.experimental.pallas import tpu as pltpu
from jax.sharding import PartitionSpec as P

beta_first = 0.9
beta_second = 0.999
learn_rate = 0.01
adam_eps = 1e-08

MESH = pl.DeviceIdType.MESH
VMEM = pl.BlockSpec(memory_space=pltpu.VMEM)
RING = 4
CORES = 2
HALVES = 2
NODES = RING * HALVES


def silu_value(values):
    return values * jax.nn.sigmoid(values)


def contract_rows(left, right):
    return lax.dot_general(
        left, right, (((0,), (0,)), ((), ())), preferred_element_type=jnp.float32
    )


def place():
    dp, ex = lax.axis_index("dp"), lax.axis_index("expert")
    return dp, ex, dp // (RING * CORES), (dp // CORES) % RING, dp % CORES


def index_of(z, y, core):
    return ((z % RING) * RING + y % RING) * CORES + core


def send(src, dst, send_sem, recv_sem, device):
    return pltpu.make_async_remote_copy(
        src_ref=src,
        dst_ref=dst,
        send_sem=send_sem,
        recv_sem=recv_sem,
        device_id=device,
        device_id_type=MESH,
    )


def greet(devices, experts, dp, ex):
    barrier = pltpu.get_barrier_semaphore()
    for device in devices:
        pl.semaphore_signal(barrier, inc=1, device_id=device, device_id_type=MESH)

    def one(step, carry):
        pl.semaphore_signal(
            barrier, inc=1, device_id=(dp, (ex + step) % experts), device_id_type=MESH
        )
        return carry

    lax.fori_loop(1, experts, one, 0)
    return lambda: pl.semaphore_wait(barrier, len(devices) + experts - 1)


def exchange(hosts, dp, ex, src, dst, send_sems, recv_sems):
    me, first = ex % hosts, ex - ex % hosts

    def copy(step):
        target = (me + step) % hosts
        return send(
            src.at[:, target],
            dst.at[:, me],
            send_sems.at[target],
            recv_sems.at[me],
            (dp, first + target),
        )

    def start(step, carry):
        copy(step).start()
        return carry

    def arrival(step, carry):
        other = (me + step) % hosts
        there = dst.at[:, other]
        send(
            there, there, send_sems.at[other], recv_sems.at[other], (dp, first + other)
        ).wait_recv()
        return carry

    def departure(step, carry):
        copy(step).wait_send()
        return carry

    lax.fori_loop(1, hosts, start, 0)
    for half in range(HALVES):
        dst[half, me] = src[half, me]
    return (
        lambda: lax.fori_loop(1, hosts, arrival, 0),
        lambda: lax.fori_loop(1, hosts, departure, 0),
    )


def middle(q, core):
    z = 2 + 2 * (q // RING)
    return (z + core * (7 - 2 * z)) * RING + q % RING


def middle_of(ex, core):
    z = ex // RING
    z = z + core * (7 - 2 * z)
    return (z % 2 == 0) & (z >= 2), (z // 2 - 1) * RING + ex % RING


def layer_kernel(
    experts,
    place_ref,
    pick_ref,
    gates_ref,
    tokens_ref,
    cot_ref,
    weight_ref,
    master_ref,
    first_ref,
    second_ref,
    source_ref,
    combined_ref,
    gate_grads_ref,
    grads_ref,
    new_master_ref,
    new_first_ref,
    new_second_ref,
    whole,
    whole_down,
    pack,
    rows,
    rows_up,
    both,
    hidden,
    in_from,
    in_to,
    up_from,
    up_to,
    out_from,
    out_to,
    partial,
    c_buf,
    y_from,
    y_buf,
    z_own,
    z_from,
    z_buf,
    state,
    spread,
    ordered,
    arrived,
    local_sem,
    in_send,
    in_recv,
    up_send,
    up_recv,
    out_send,
    out_recv,
    wz_send,
    wz_recv,
    wy_send,
    wy_recv,
    wc_send,
    wc_recv,
    dz_send,
    dz_recv,
    dy_send,
    dy_recv,
    dc_send,
    dc_recv,
    c_send,
    c_recv,
    y_send,
    y_recv,
    z_send,
    z_recv,
    s_send,
    s_recv,
    t_send,
    t_recv,
):
    dp, ex, z, y, core = place()
    sibling = (index_of(z, y, 1 - core), ex)
    ring_y = [(index_of(z, y + s, core), ex) for s in range(1, RING)]
    hosts = experts // HALVES
    node = z * HALVES + ex // hosts

    def at_node(step):
        other = (node + step + NODES) % NODES
        return (index_of(other // HALVES, y, core), other % HALVES * hosts + ex % hosts)

    right, left = at_node(1), at_node(-1)
    outer = at_node(2 * (ex // hosts) - 1)
    all_here = greet([sibling, outer] + ring_y, experts, dp, ex)

    slots, model = rows.shape
    depth = weight_ref.shape[0]
    ff = hidden.shape[1]
    lanes = pack.shape[1]
    per_row = model // lanes
    block = in_from.shape[2]
    part_rows = slots // HALVES
    quarter = model // RING
    group = per_row // RING

    def columns(i, width):
        return pl.ds(pl.multiple_of(i * width, width), width)

    def pack_columns(i, value):
        for c in range(group):
            pack[pl.ds(i * group + c, slots, stride=per_row), :] = value[
                :, c * lanes : (c + 1) * lanes
            ]

    def to_blocks(dst):
        for half in range(HALVES):
            value = pack[pl.ds(half * hosts * block, hosts * block), :].astype(dst.dtype)
            dst[half] = value.reshape((hosts, block, lanes))

    def to_rows(src, dst):
        for half in range(HALVES):
            value = src[half].astype(jnp.float32)
            pack[pl.ds(half * hosts * block, hosts * block), :] = value.reshape(
                (hosts * block, lanes)
            )

        def other(i, carry):
            for c in range(group):
                value = pack[pl.ds(i * group + c, slots, stride=per_row), :]
                dst[:, columns(i * group + c, lanes)] = value.astype(dst.dtype)
            return carry

        lax.fori_loop(0, RING, other, 0)

    def place_in(i, carry):
        value = tokens_ref[:, columns(i, quarter)]
        pack_columns(i, jnp.dot(place_ref[...], value, preferred_element_type=jnp.float32))
        return carry

    def place_up(i, carry):
        value = gates_ref[...] * cot_ref[:, columns(i, quarter)].astype(jnp.float32)
        value = value.astype(cot_ref.dtype)
        pack_columns(i, jnp.dot(place_ref[...], value, preferred_element_type=jnp.float32))
        return carry

    lax.fori_loop(0, RING, place_in, 0)
    to_blocks(in_from)
    all_here()

    sent = []

    def start(copy):
        copy.start()
        sent.append(copy)

    nodes = [(node + step + NODES) % NODES for step in (0, -1, 1, -2, 2, -3, 3, 4)]
    half = depth // 2
    every, low, high = (0, depth), (0, half), (half, half)

    def gather(src, dst, zs, zr, ys, yr, cs, cr):
        def slot(k, first=0, count=depth, y=y, core=core):
            row = index_of(nodes[k] // HALVES, y, core) * depth + first
            return dst.at[nodes[k] % HALVES, pl.ds(pl.multiple_of(row, half), count), :]

        def z_copy(i, from_ref, k, part, device):
            return send(from_ref, slot(k, *part), zs.at[i], zr.at[i], device)

        def z_arrival(i, k, part=every):
            there = slot(k, *part)
            send(there, there, zs.at[i], zr.at[i], right).wait_recv()

        def spread_weight(k, from_ref):
            for s in range(1, RING):
                start(
                    send(from_ref, slot(k), ys.at[k, s - 1], yr.at[k, s - 1], ring_y[s - 1])
                )
            start(send(from_ref, slot(k), cs.at[k, 0], cr.at[k, 0], sibling))

        def begin():
            start(z_copy(0, src, 0, every, right))
            start(z_copy(1, src, 0, every, left))
            spread_weight(0, src)

        def arrive(step):
            from_left, from_right = 2 * step - 1, 2 * step
            part = every if step < 3 else low
            z_arrival(2 * step - 2, from_left)
            start(z_copy(2 * step, slot(from_left, *part), from_left, part, right))
            part = every if step < 3 else high
            z_arrival(2 * step - 1, from_right)
            start(z_copy(2 * step + 1, slot(from_right, *part), from_right, part, left))
            spread_weight(from_left, slot(from_left))
            spread_weight(from_right, slot(from_right))

        def opposite():
            z_arrival(6, 7, low)
            z_arrival(7, 7, high)
            spread_weight(7, slot(7))

        def pass_on(k):
            for s in range(1, RING):
                there = slot(k, y=y + RING - s)
                send(there, there, ys.at[k, s - 1], yr.at[k, s - 1], sibling).wait_recv()
                start(send(there, there, cs.at[k, s], cr.at[k, s], sibling))

        def complete(k):
            for s in range(RING):
                there = slot(k, y=y + RING - s, core=1 - core)
                send(there, there, cs.at[k, s], cr.at[k, s], sibling).wait_recv()

        own = pltpu.make_async_copy(src, slot(0), local_sem.at[0 if dst is whole else 1])
        return own, begin, arrive, opposite, pass_on, complete

    gate_up = gather(
        weight_ref.at[:, pl.ds(0, 2 * ff)],
        whole,
        wz_send,
        wz_recv,
        wy_send,
        wy_recv,
        wc_send,
        wc_recv,
    )
    down = gather(
        weight_ref.at[:, pl.ds(2 * ff, ff)],
        whole_down,
        dz_send,
        dz_recv,
        dy_send,
        dy_recv,
        dc_send,
        dc_recv,
    )
    own, begin, arrive, opposite, pass_on, complete = gate_up
    begin()
    in_there, in_left = exchange(hosts, dp, ex, in_from, in_to, in_send, in_recv)
    own.start()
    lax.fori_loop(0, RING, place_up, 0)
    to_blocks(up_from)
    up_there, up_left = exchange(hosts, dp, ex, up_from, up_to, up_send, up_recv)
    both[...] = jnp.zeros_like(both)

    def rows_of(half):
        return pl.ds(pl.multiple_of(half * part_rows, part_rows), part_rows)

    def multiply(k):
        complete(k)
        half, part = nodes[k] % HALVES, columns(nodes[k] // HALVES, quarter)
        these = rows_of(half)
        both[these, :] += jnp.dot(
            rows[these, part], whole[half, part, :], preferred_element_type=jnp.float32
        )

    arrive(1)
    pass_on(0)
    arrive(2)
    pass_on(1)
    pass_on(2)
    in_there()
    to_rows(in_to, rows)
    own.wait()
    arrive(3)
    pass_on(3)
    pass_on(4)
    multiply(0)
    multiply(1)
    multiply(2)
    opposite()
    pass_on(5)
    pass_on(6)
    multiply(3)
    multiply(4)
    multiply(5)
    multiply(6)
    pass_on(7)
    up_there()
    to_rows(up_to, rows_up)
    multiply(7)
    own, begin, arrive, opposite, pass_on, complete = down
    begin()
    own.start()
    hidden[...] = (silu_value(both[:, :ff]) * both[:, ff:]).astype(hidden.dtype)

    def grad(i, carry):
        for half in range(HALVES):
            these = pl.ds(half * part_rows, part_rows)
            value = contract_rows(rows_up[these, columns(i, quarter)], hidden[these, :])
            partial[half, pl.ds(i * RING, RING)] = value.astype(partial.dtype).reshape(
                (RING, CORES, depth, ff)
            )
        return carry

    lax.fori_loop(0, RING, grad, 0)
    to_core = send(partial.at[:, :, 1 - core], c_buf, c_send, c_recv, sibling)
    to_core.start()
    to_core.wait()

    def pair(i, carry):
        at, row = i // RING, i % RING
        for half in range(HALVES):
            y_from[row, half, at] = (
                partial[half, i, core].astype(jnp.float32) + c_buf[half, i].astype(jnp.float32)
            ).astype(y_from.dtype)
        return carry

    lax.fori_loop(0, RING * RING, pair, 0)
    y_copies = [
        send(
            y_from.at[(y + s) % RING],
            y_buf.at[s - 1],
            y_send.at[s - 1],
            y_recv.at[s - 1],
            ring_y[s - 1],
        )
        for s in range(1, RING)
    ]
    for copy in y_copies:
        copy.start()
    arrive(1)
    pass_on(0)
    for copy in y_copies:
        copy.wait()

    def quad(i, carry):
        for part in range(HALVES):
            total = y_from[y, part, i].astype(jnp.float32)
            for s in range(RING - 1):
                total += y_buf[s, part, i].astype(jnp.float32)
            z_own[i * HALVES + part] = total
        return carry

    lax.fori_loop(0, RING, quad, 0)

    def mine(step):
        return z_own[(node + step + NODES) % NODES]

    def ring_copy(step, way):
        rows_sent = pl.ds(way * half, half) if step == 0 else pl.ds(0, depth)
        return send(
            z_from.at[way, step, rows_sent],
            z_buf.at[way, step, rows_sent],
            z_send.at[way, step],
            z_recv.at[way, step],
            (right, left)[way],
        )

    def ring_step(step):
        for way in range(2):
            total = mine((NODES // 2 - step) * (1 - 2 * way))
            if step == 0:
                cut = slice(way * half, way * half + half)
                z_from[way, step, cut, :] = total[cut].astype(z_from.dtype)
            elif step == 1:
                ring_copy(0, way).wait_recv()
                here, there = (0, half) if way == 0 else (half, 0)
                z_from[way, step, here : here + half, :] = (
                    total[here : here + half]
                    + z_buf[way, 0, here : here + half, :].astype(jnp.float32)
                ).astype(z_from.dtype)
                z_from[way, step, there : there + half, :] = total[there : there + half].astype(
                    z_from.dtype
                )
            else:
                ring_copy(step - 1, way).wait_recv()
                z_from[way, step] = (total + z_buf[way, step - 1].astype(jnp.float32)).astype(
                    z_from.dtype
                )
            ring_copy(step, way).start()

    last = NODES // 2 - 1
    ring_step(0)
    arrive(2)
    ring_step(1)
    pass_on(1)
    pass_on(2)
    ring_step(2)
    arrive(3)
    pass_on(3)
    pass_on(4)
    ring_step(3)
    opposite()
    pass_on(5)
    pass_on(6)
    for way in range(2):
        ring_copy(last, way).wait_recv()
    grads = mine(0) + z_buf[0, last].astype(jnp.float32) + z_buf[1, last].astype(jnp.float32)
    grads_ref[...] = grads
    first = beta_first * first_ref[...] + (1.0 - beta_first) * grads
    second = beta_second * second_ref[...] + (1.0 - beta_second) * grads * grads
    updated = master_ref[...] - learn_rate * first / (jnp.sqrt(second) + adam_eps)
    tall, wide = state.shape[2:]
    pieces = state.shape[0]
    across = grads.shape[1] // wide

    def piece(q):
        return pl.ds(q // across * tall, tall), pl.ds(q % across * wide, wide)

    for i, value in enumerate((updated, first, second)):
        value = value.astype(state.dtype)
        for q in range(pieces):
            row, column = q // across * tall, q % across * wide
            state[q, i] = value[row : row + tall, column : column + wide]

    is_middle, held = middle_of(ex, core)

    def spread_copy(q):
        return send(
            state.at[q], spread.at[ex], s_send.at[q], s_recv.at[ex], (dp, middle(q, core))
        )

    for q in range(pieces):

        @pl.when(middle(q, core) != ex)
        def _(q=q):
            spread_copy(q).start()

    def order_copy(step):
        target = (ex + step) % experts
        return send(
            ordered.at[target], arrived.at[held], t_send.at[target], t_recv.at[held], (dp, target)
        )

    pass_on(7)
    for k in range(NODES):
        complete(k)
    own.wait()

    def outputs(i, carry):
        for part in range(HALVES):
            value = lax.dot_general(
                hidden[pl.ds(part * part_rows, part_rows), :],
                whole_down[part, columns(i, quarter), :],
                (((1,), (1,)), ((), ())),
                preferred_element_type=jnp.float32,
            )
            for c in range(group):
                first_row = part * part_rows * per_row + i * group + c
                pack[pl.ds(first_row, part_rows, stride=per_row), :] = value[
                    :, c * lanes : (c + 1) * lanes
                ]
        return carry

    lax.fori_loop(0, RING, outputs, 0)
    to_blocks(out_from)
    out_there, out_left = exchange(hosts, dp, ex, out_from, out_to, out_send, out_recv)

    @pl.when(is_middle)
    def _():
        spread[ex] = state[held]

        def landed(step, carry):
            other = (ex + step) % experts
            there = spread.at[other]
            send(there, there, s_send.at[0], s_recv.at[other], (dp, other)).wait_recv()
            return carry

        def pick(e, carry):
            ordered[e] = spread[source_ref[e]]
            return carry

        def start(step, carry):
            order_copy(step).start()
            return carry

        lax.fori_loop(1, experts, landed, 0)
        lax.fori_loop(0, experts, pick, 0)
        lax.fori_loop(1, experts, start, 0)
        arrived[held] = ordered[ex]

    out_there()
    to_rows(out_to, rows)

    def combine(i, total):
        part = columns(i, quarter)
        value = jnp.dot(pick_ref[...], rows[:, part], preferred_element_type=jnp.float32)
        combined_ref[:, part] = (gates_ref[...] * value).astype(combined_ref.dtype)
        return total + cot_ref[:, part].astype(jnp.float32) * value

    total = lax.fori_loop(
        0, RING, combine, jnp.zeros((tokens_ref.shape[0], quarter), jnp.float32)
    )
    gate_grads_ref[...] = jnp.sum(total, axis=1, keepdims=True)

    for q in range(pieces):
        there = arrived.at[q]

        @pl.when(middle(q, core) != ex)
        def _(q=q, there=there):
            spread_copy(q).wait_send()
            send(
                there, there, t_send.at[0], t_recv.at[q], (dp, middle(q, core))
            ).wait_recv()

    for q in range(pieces):
        for i, ref in enumerate((new_master_ref, new_first_ref, new_second_ref)):
            ref[piece(q)] = arrived[q, i].astype(ref.dtype)

    @pl.when(is_middle)
    def _():
        def sent(step, carry):
            order_copy(step).wait_send()
            return carry

        lax.fori_loop(1, experts, sent, 0)

    for copy in sent:
        copy.wait_send()
    for step in range(last + 1):
        for way in range(2):
            ring_copy(step, way).wait_send()
    in_left()
    up_left()
    out_left()


def layer(place_slots, gates, tokens, cotangent, weight, state, source):
    slots, tok_rows = place_slots.shape
    model = tokens.shape[1]
    experts = source.shape[0]
    depth, ff = weight.shape[0], weight.shape[1] // 3
    dma = pltpu.SemaphoreType.DMA
    kind = tokens.dtype
    lanes = 128
    hosts = experts // HALVES
    packed = (HALVES, hosts, slots * model // lanes // experts, lanes)
    block = (depth, ff)
    piece = (3, 16, 128)
    pieces = depth * ff // (16 * 128)

    def sixteen(*shape):
        return pltpu.VMEM(shape, kind)

    return pl.pallas_call(
        functools.partial(layer_kernel, experts),
        out_shape=[
            jax.ShapeDtypeStruct(tokens.shape, kind),
            jax.ShapeDtypeStruct((tok_rows, 1), jnp.float32),
        ]
        + [jax.ShapeDtypeStruct(block, jnp.float32)] * 4,
        in_specs=[VMEM] * 9 + [pl.BlockSpec(memory_space=pltpu.SMEM)],
        out_specs=[VMEM] * 6,
        scratch_shapes=[
            sixteen(HALVES, model, 2 * ff),
            sixteen(HALVES, model, ff),
            pltpu.VMEM((slots * model // lanes, lanes), jnp.float32),
            sixteen(slots, model),
            sixteen(slots, model),
            pltpu.VMEM((slots, 2 * ff), jnp.float32),
            sixteen(slots, ff),
        ]
        + [sixteen(*packed)] * 6
        + [
            sixteen(HALVES, RING * RING, CORES, *block),
            sixteen(HALVES, RING * RING, *block),
            sixteen(RING, HALVES, RING, *block),
            sixteen(RING - 1, HALVES, RING, *block),
            pltpu.VMEM((NODES,) + block, jnp.float32),
            sixteen(2, NODES // 2, *block),
            sixteen(2, NODES // 2, *block),
            sixteen(pieces, *piece),
            sixteen(experts, *piece),
            sixteen(experts, *piece),
            sixteen(pieces, *piece),
            dma((2,)),
        ]
        + [dma((hosts,))] * 6
        + ([dma((NODES,))] * 2 + [dma((NODES, RING - 1))] * 2 + [dma((NODES, RING))] * 2) * 2
        + [dma] * 2
        + [dma((RING - 1,))] * 2
        + [dma((2, NODES // 2))] * 2
        + [dma((pieces,)), dma((experts,)), dma((experts,)), dma((pieces,))],
        compiler_params=pltpu.CompilerParams(
            collective_id=0, has_side_effects=True, vmem_limit_bytes=48 * 1024 * 1024
        ),
        name="layer",
    )(place_slots, place_slots.T, gates, tokens, cotangent, weight, *state, source)


def shards(
    tokens,
    route_ids,
    route_gates,
    cotangent,
    expert_weights,
    master,
    first_moment,
    second_moment,
    old_place,
    new_place,
):
    experts = lax.axis_size("expert")
    tok_rows = tokens.shape[0]
    routes = route_ids.shape[1]
    capacity = 5 * tok_rows * routes // (4 * experts)
    slots = experts * capacity
    expert_range = jnp.arange(experts, dtype=jnp.int32)
    holder = jnp.sum(
        expert_range[None, :] * (old_place[None, :] == expert_range[:, None]).astype(jnp.int32),
        axis=1,
    )
    flat_ids = route_ids.reshape(-1)
    onehot = (flat_ids[:, None] == expert_range[None, :]).astype(jnp.int32)
    rank_in = jnp.sum((jnp.cumsum(onehot, axis=0) - onehot) * onehot, axis=1)
    target = jnp.sum(onehot * holder[None, :], axis=1)
    slot_index = target * capacity + rank_in
    slot_range = jnp.arange(slots, dtype=jnp.int32)
    place_pairs = (slot_range[:, None] == slot_index[None, :]).astype(jnp.bfloat16)
    source_slot = jnp.sum(
        expert_range[None, :] * (old_place[None, :] == new_place[:, None]).astype(jnp.int32), axis=1
    )
    combined, gate_grads, *state = layer(
        place_pairs,
        route_gates,
        tokens,
        cotangent,
        expert_weights[0],
        (master[0], first_moment[0], second_moment[0]),
        source_slot,
    )
    return (combined, gate_grads) + tuple(value[None] for value in state)


def solution(mesh):
    in_specs = (
        P(("dp", "expert"), None),
        P(("dp", "expert"), None),
        P(("dp", "expert"), None),
        P(("dp", "expert"), None),
        P("expert", "dp", None),
        P("expert", "dp", None),
        P("expert", "dp", None),
        P("expert", "dp", None),
        P(),
        P(),
    )
    out_specs = (
        P(("dp", "expert"), None),
        P(("dp", "expert"), None),
        P("expert", "dp", None),
        P("expert", "dp", None),
        P("expert", "dp", None),
        P("expert", "dp", None),
    )
    return jax.shard_map(shards, mesh=mesh, in_specs=in_specs, out_specs=out_specs, check_vma=False)
```

```python
import functools

import jax
import jax.numpy as jnp
from jax import lax
from jax.experimental import pallas as pl
from jax.experimental.pallas import tpu as pltpu
from jax.sharding import PartitionSpec as P

beta_first = 0.9
beta_second = 0.999
learn_rate = 0.01
adam_eps = 1e-08

MESH = pl.DeviceIdType.MESH
VMEM = pl.BlockSpec(memory_space=pltpu.VMEM)
RING = 4
CORES = 2
HALVES = 2
NODES = RING * HALVES


def silu_value(values):
    return values * jax.nn.sigmoid(values)


def contract_rows(left, right):
    return lax.dot_general(
        left, right, (((0,), (0,)), ((), ())), preferred_element_type=jnp.float32
    )


def place():
    dp, ex = lax.axis_index("dp"), lax.axis_index("expert")
    return dp, ex, dp // (RING * CORES), (dp // CORES) % RING, dp % CORES


def index_of(z, y, core):
    return ((z % RING) * RING + y % RING) * CORES + core


def send(src, dst, send_sem, recv_sem, device):
    return pltpu.make_async_remote_copy(
        src_ref=src,
        dst_ref=dst,
        send_sem=send_sem,
        recv_sem=recv_sem,
        device_id=device,
        device_id_type=MESH,
    )


def greet(devices, experts, dp, ex):
    barrier = pltpu.get_barrier_semaphore()
    for device in devices:
        pl.semaphore_signal(barrier, inc=1, device_id=device, device_id_type=MESH)

    def one(step, carry):
        pl.semaphore_signal(
            barrier, inc=1, device_id=(dp, (ex + step) % experts), device_id_type=MESH
        )
        return carry

    lax.fori_loop(1, experts, one, 0)
    return lambda: pl.semaphore_wait(barrier, len(devices) + experts - 1)


def exchange(hosts, dp, ex, src, dst, send_sems, recv_sems):
    me, first = ex % hosts, ex - ex % hosts

    def copy(step):
        target = (me + step) % hosts
        return send(
            src.at[:, target],
            dst.at[:, me],
            send_sems.at[target],
            recv_sems.at[me],
            (dp, first + target),
        )

    def start(step, carry):
        copy(step).start()
        return carry

    def arrival(step, carry):
        other = (me + step) % hosts
        there = dst.at[:, other]
        send(
            there, there, send_sems.at[other], recv_sems.at[other], (dp, first + other)
        ).wait_recv()
        return carry

    def departure(step, carry):
        copy(step).wait_send()
        return carry

    lax.fori_loop(1, hosts, start, 0)
    for half in range(HALVES):
        dst[half, me] = src[half, me]
    return (
        lambda: lax.fori_loop(1, hosts, arrival, 0),
        lambda: lax.fori_loop(1, hosts, departure, 0),
    )


def middle(q, core):
    z = 2 + 2 * (q // RING)
    return (z + core * (7 - 2 * z)) * RING + q % RING


def middle_of(ex, core):
    z = ex // RING
    z = z + core * (7 - 2 * z)
    return (z % 2 == 0) & (z >= 2), (z // 2 - 1) * RING + ex % RING


def layer_kernel(
    experts,
    place_ref,
    pick_ref,
    gates_ref,
    tokens_ref,
    cot_ref,
    weight_ref,
    master_ref,
    first_ref,
    second_ref,
    source_ref,
    combined_ref,
    gate_grads_ref,
    grads_ref,
    new_master_ref,
    new_first_ref,
    new_second_ref,
    whole,
    whole_down,
    pack,
    rows,
    rows_up,
    both,
    hidden,
    in_from,
    in_to,
    up_from,
    up_to,
    out_from,
    out_to,
    partial,
    c_buf,
    y_from,
    y_buf,
    z_own,
    z_from,
    z_buf,
    state,
    spread,
    ordered,
    arrived,
    local_sem,
    in_send,
    in_recv,
    up_send,
    up_recv,
    out_send,
    out_recv,
    wz_send,
    wz_recv,
    wy_send,
    wy_recv,
    wc_send,
    wc_recv,
    dz_send,
    dz_recv,
    dy_send,
    dy_recv,
    dc_send,
    dc_recv,
    c_send,
    c_recv,
    y_send,
    y_recv,
    z_send,
    z_recv,
    s_send,
    s_recv,
    t_send,
    t_recv,
):
    dp, ex, z, y, core = place()
    sibling = (index_of(z, y, 1 - core), ex)
    ring_y = [(index_of(z, y + s, core), ex) for s in range(1, RING)]
    hosts = experts // HALVES
    node = z * HALVES + ex // hosts

    def at_node(step):
        other = (node + step + NODES) % NODES
        return (index_of(other // HALVES, y, core), other % HALVES * hosts + ex % hosts)

    right, left = at_node(1), at_node(-1)
    outer = at_node(2 * (ex // hosts) - 1)
    all_here = greet([sibling, outer] + ring_y, experts, dp, ex)

    slots, model = rows.shape
    depth = weight_ref.shape[0]
    ff = hidden.shape[1]
    lanes = pack.shape[1]
    per_row = model // lanes
    block = in_from.shape[2]
    part_rows = slots // HALVES
    quarter = model // RING
    group = per_row // RING

    def columns(i, width):
        return pl.ds(pl.multiple_of(i * width, width), width)

    def pack_columns(i, value):
        for c in range(group):
            pack[pl.ds(i * group + c, slots, stride=per_row), :] = value[
                :, c * lanes : (c + 1) * lanes
            ]

    def to_blocks(dst):
        for half in range(HALVES):
            value = pack[pl.ds(half * hosts * block, hosts * block), :].astype(dst.dtype)
            dst[half] = value.reshape((hosts, block, lanes))

    def to_rows(src, dst):
        for half in range(HALVES):
            value = src[half].astype(jnp.float32)
            pack[pl.ds(half * hosts * block, hosts * block), :] = value.reshape(
                (hosts * block, lanes)
            )

        def other(i, carry):
            for c in range(group):
                value = pack[pl.ds(i * group + c, slots, stride=per_row), :]
                dst[:, columns(i * group + c, lanes)] = value.astype(dst.dtype)
            return carry

        lax.fori_loop(0, RING, other, 0)

    def place_in(i, carry):
        value = tokens_ref[:, columns(i, quarter)]
        pack_columns(i, jnp.dot(place_ref[...], value, preferred_element_type=jnp.float32))
        return carry

    def place_up(i, carry):
        value = gates_ref[...] * cot_ref[:, columns(i, quarter)].astype(jnp.float32)
        value = value.astype(cot_ref.dtype)
        pack_columns(i, jnp.dot(place_ref[...], value, preferred_element_type=jnp.float32))
        return carry

    lax.fori_loop(0, RING, place_in, 0)
    to_blocks(in_from)
    all_here()

    sent = []

    def start(copy):
        copy.start()
        sent.append(copy)

    nodes = [(node + step + NODES) % NODES for step in (0, -1, 1, -2, 2, -3, 3, 4)]
    half = depth // 2
    every, low, high = (0, depth), (0, half), (half, half)

    def gather(src, dst, zs, zr, ys, yr, cs, cr):
        def slot(k, first=0, count=depth, y=y, core=core):
            row = index_of(nodes[k] // HALVES, y, core) * depth + first
            return dst.at[nodes[k] % HALVES, pl.ds(pl.multiple_of(row, half), count), :]

        def z_copy(i, from_ref, k, part, device):
            return send(from_ref, slot(k, *part), zs.at[i], zr.at[i], device)

        def z_arrival(i, k, part=every):
            there = slot(k, *part)
            send(there, there, zs.at[i], zr.at[i], right).wait_recv()

        def spread_weight(k, from_ref):
            for s in range(1, RING):
                start(
                    send(from_ref, slot(k), ys.at[k, s - 1], yr.at[k, s - 1], ring_y[s - 1])
                )
            start(send(from_ref, slot(k), cs.at[k, 0], cr.at[k, 0], sibling))

        def begin():
            start(z_copy(0, src, 0, every, right))
            start(z_copy(1, src, 0, every, left))

        def begin_across():
            spread_weight(0, src)

        def arrive(step):
            from_left, from_right = 2 * step - 1, 2 * step
            part = every if step < 3 else low
            z_arrival(2 * step - 2, from_left)
            start(z_copy(2 * step, slot(from_left, *part), from_left, part, right))
            part = every if step < 3 else high
            z_arrival(2 * step - 1, from_right)
            start(z_copy(2 * step + 1, slot(from_right, *part), from_right, part, left))
            spread_weight(from_left, slot(from_left))
            spread_weight(from_right, slot(from_right))

        def opposite():
            z_arrival(6, 7, low)
            z_arrival(7, 7, high)
            spread_weight(7, slot(7))

        def pass_on(k):
            for s in range(1, RING):
                there = slot(k, y=y + RING - s)
                send(there, there, ys.at[k, s - 1], yr.at[k, s - 1], sibling).wait_recv()
                start(send(there, there, cs.at[k, s], cr.at[k, s], sibling))

        def complete(k):
            for s in range(RING):
                there = slot(k, y=y + RING - s, core=1 - core)
                send(there, there, cs.at[k, s], cr.at[k, s], sibling).wait_recv()

        own = pltpu.make_async_copy(src, slot(0), local_sem.at[0 if dst is whole else 1])
        return own, begin, begin_across, arrive, opposite, pass_on, complete

    gate_up = gather(
        weight_ref.at[:, pl.ds(0, 2 * ff)],
        whole,
        wz_send,
        wz_recv,
        wy_send,
        wy_recv,
        wc_send,
        wc_recv,
    )
    down = gather(
        weight_ref.at[:, pl.ds(2 * ff, ff)],
        whole_down,
        dz_send,
        dz_recv,
        dy_send,
        dy_recv,
        dc_send,
        dc_recv,
    )
    own, begin, begin_across, arrive, opposite, pass_on, complete = gate_up
    begin()
    begin_across()
    in_there, in_left = exchange(hosts, dp, ex, in_from, in_to, in_send, in_recv)
    own.start()
    lax.fori_loop(0, RING, place_up, 0)
    to_blocks(up_from)
    both[...] = jnp.zeros_like(both)

    def rows_of(half):
        return pl.ds(pl.multiple_of(half * part_rows, part_rows), part_rows)

    def multiply(k):
        complete(k)
        half, part = nodes[k] % HALVES, columns(nodes[k] // HALVES, quarter)
        these = rows_of(half)
        both[these, :] += jnp.dot(
            rows[these, part], whole[half, part, :], preferred_element_type=jnp.float32
        )

    arrive(1)
    up_there, up_left = exchange(hosts, dp, ex, up_from, up_to, up_send, up_recv)
    pass_on(0)
    arrive(2)
    pass_on(1)
    pass_on(2)
    in_there()
    to_rows(in_to, rows)
    own.wait()
    arrive(3)
    pass_on(3)
    pass_on(4)
    multiply(0)
    multiply(1)
    multiply(2)
    opposite()
    begin_down = down[1]
    begin_down()
    pass_on(5)
    pass_on(6)
    multiply(3)
    multiply(4)
    multiply(5)
    multiply(6)
    pass_on(7)
    up_there()
    to_rows(up_to, rows_up)
    multiply(7)
    own, _, begin_across, arrive, opposite, pass_on, complete = down
    begin_across()
    own.start()
    hidden[...] = (silu_value(both[:, :ff]) * both[:, ff:]).astype(hidden.dtype)

    def grad(i, carry):
        for half in range(HALVES):
            these = pl.ds(half * part_rows, part_rows)
            value = contract_rows(rows_up[these, columns(i, quarter)], hidden[these, :])
            partial[half, pl.ds(i * RING, RING)] = value.astype(partial.dtype).reshape(
                (RING, CORES, depth, ff)
            )
        return carry

    lax.fori_loop(0, RING, grad, 0)
    to_core = send(partial.at[:, :, 1 - core], c_buf, c_send, c_recv, sibling)
    to_core.start()
    to_core.wait()

    def pair(i, carry):
        at, row = i // RING, i % RING
        for half in range(HALVES):
            y_from[row, half, at] = (
                partial[half, i, core].astype(jnp.float32) + c_buf[half, i].astype(jnp.float32)
            ).astype(y_from.dtype)
        return carry

    lax.fori_loop(0, RING * RING, pair, 0)
    order = (4, 3, -3, 2, -2, 1, -1, 0)
    targets = [(node + step + NODES) % NODES for step in order]

    def y_copy(k, s):
        at = (targets[k] % HALVES, targets[k] // HALVES)
        return send(
            y_from.at[(y + s) % RING, at[0], at[1]],
            y_buf.at[s - 1, at[0], at[1]],
            y_send.at[k, s - 1],
            y_recv.at[k, s - 1],
            ring_y[s - 1],
        )

    for k in range(NODES):
        for s in range(1, RING):
            y_copy(k, s).start()

    def y_sum(k):
        part, at = targets[k] % HALVES, targets[k] // HALVES
        total = y_from[y, part, at].astype(jnp.float32)
        for s in range(1, RING):
            y_copy(k, s).wait_recv()
            total += y_buf[s - 1, part, at].astype(jnp.float32)
        z_own[targets[k]] = total

    def mine(step):
        return z_own[(node + step + NODES) % NODES]

    def ring_copy(step, way):
        rows_sent = pl.ds(way * half, half) if step == 0 else pl.ds(0, depth)
        return send(
            z_from.at[way, step, rows_sent],
            z_buf.at[way, step, rows_sent],
            z_send.at[way, step],
            z_recv.at[way, step],
            (right, left)[way],
        )

    def ring_step(step):
        for way in range(2):
            total = mine((NODES // 2 - step) * (1 - 2 * way))
            if step == 0:
                cut = slice(way * half, way * half + half)
                z_from[way, step, cut, :] = total[cut].astype(z_from.dtype)
            elif step == 1:
                ring_copy(0, way).wait_recv()
                here, there = (0, half) if way == 0 else (half, 0)
                z_from[way, step, here : here + half, :] = (
                    total[here : here + half]
                    + z_buf[way, 0, here : here + half, :].astype(jnp.float32)
                ).astype(z_from.dtype)
                z_from[way, step, there : there + half, :] = total[there : there + half].astype(
                    z_from.dtype
                )
            else:
                ring_copy(step - 1, way).wait_recv()
                z_from[way, step] = (total + z_buf[way, step - 1].astype(jnp.float32)).astype(
                    z_from.dtype
                )
            ring_copy(step, way).start()

    last = NODES // 2 - 1
    y_sum(0)
    ring_step(0)
    arrive(1)
    pass_on(0)
    y_sum(1)
    y_sum(2)
    ring_step(1)
    arrive(2)
    y_sum(3)
    y_sum(4)
    ring_step(2)
    pass_on(1)
    pass_on(2)
    arrive(3)
    y_sum(5)
    y_sum(6)
    ring_step(3)
    pass_on(3)
    pass_on(4)
    opposite()
    pass_on(5)
    pass_on(6)
    y_sum(7)
    for way in range(2):
        ring_copy(last, way).wait_recv()
    grads = mine(0) + z_buf[0, last].astype(jnp.float32) + z_buf[1, last].astype(jnp.float32)
    grads_ref[...] = grads
    first = beta_first * first_ref[...] + (1.0 - beta_first) * grads
    second = beta_second * second_ref[...] + (1.0 - beta_second) * grads * grads
    updated = master_ref[...] - learn_rate * first / (jnp.sqrt(second) + adam_eps)
    tall, wide = state.shape[2:]
    pieces = state.shape[0]
    across = grads.shape[1] // wide

    def piece(q):
        return pl.ds(q // across * tall, tall), pl.ds(q % across * wide, wide)

    for i, value in enumerate((updated, first, second)):
        value = value.astype(state.dtype)
        for q in range(pieces):
            row, column = q // across * tall, q % across * wide
            state[q, i] = value[row : row + tall, column : column + wide]

    is_middle, held = middle_of(ex, core)

    def spread_copy(q):
        return send(
            state.at[q], spread.at[ex], s_send.at[q], s_recv.at[ex], (dp, middle(q, core))
        )

    for q in range(pieces):

        @pl.when(middle(q, core) != ex)
        def _(q=q):
            spread_copy(q).start()

    def order_copy(step):
        target = (ex + step) % experts
        return send(
            ordered.at[target], arrived.at[held], t_send.at[target], t_recv.at[held], (dp, target)
        )

    pass_on(7)
    for k in range(NODES):
        complete(k)
    own.wait()

    def outputs(i, carry):
        for part in range(HALVES):
            value = lax.dot_general(
                hidden[pl.ds(part * part_rows, part_rows), :],
                whole_down[part, columns(i, quarter), :],
                (((1,), (1,)), ((), ())),
                preferred_element_type=jnp.float32,
            )
            for c in range(group):
                first_row = part * part_rows * per_row + i * group + c
                pack[pl.ds(first_row, part_rows, stride=per_row), :] = value[
                    :, c * lanes : (c + 1) * lanes
                ]
        return carry

    lax.fori_loop(0, RING, outputs, 0)
    to_blocks(out_from)
    out_there, out_left = exchange(hosts, dp, ex, out_from, out_to, out_send, out_recv)

    @pl.when(is_middle)
    def _():
        spread[ex] = state[held]

        def landed(step, carry):
            other = (ex + step) % experts
            there = spread.at[other]
            send(there, there, s_send.at[0], s_recv.at[other], (dp, other)).wait_recv()
            return carry

        def pick(e, carry):
            ordered[e] = spread[source_ref[e]]
            return carry

        def start(step, carry):
            order_copy(step).start()
            return carry

        lax.fori_loop(1, experts, landed, 0)
        lax.fori_loop(0, experts, pick, 0)
        lax.fori_loop(1, experts, start, 0)
        arrived[held] = ordered[ex]

    out_there()
    to_rows(out_to, rows)

    def combine(i, total):
        part = columns(i, quarter)
        value = jnp.dot(pick_ref[...], rows[:, part], preferred_element_type=jnp.float32)
        combined_ref[:, part] = (gates_ref[...] * value).astype(combined_ref.dtype)
        return total + cot_ref[:, part].astype(jnp.float32) * value

    total = lax.fori_loop(
        0, RING, combine, jnp.zeros((tokens_ref.shape[0], quarter), jnp.float32)
    )
    gate_grads_ref[...] = jnp.sum(total, axis=1, keepdims=True)

    for q in range(pieces):
        there = arrived.at[q]

        @pl.when(middle(q, core) != ex)
        def _(q=q, there=there):
            spread_copy(q).wait_send()
            send(
                there, there, t_send.at[0], t_recv.at[q], (dp, middle(q, core))
            ).wait_recv()

    for q in range(pieces):
        for i, ref in enumerate((new_master_ref, new_first_ref, new_second_ref)):
            ref[piece(q)] = arrived[q, i].astype(ref.dtype)

    @pl.when(is_middle)
    def _():
        def sent(step, carry):
            order_copy(step).wait_send()
            return carry

        lax.fori_loop(1, experts, sent, 0)

    for copy in sent:
        copy.wait_send()
    for step in range(last + 1):
        for way in range(2):
            ring_copy(step, way).wait_send()
    for k in range(NODES):
        for s in range(1, RING):
            y_copy(k, s).wait_send()
    in_left()
    up_left()
    out_left()


def layer(place_slots, gates, tokens, cotangent, weight, state, source):
    slots, tok_rows = place_slots.shape
    model = tokens.shape[1]
    experts = source.shape[0]
    depth, ff = weight.shape[0], weight.shape[1] // 3
    dma = pltpu.SemaphoreType.DMA
    kind = tokens.dtype
    lanes = 128
    hosts = experts // HALVES
    packed = (HALVES, hosts, slots * model // lanes // experts, lanes)
    block = (depth, ff)
    piece = (3, 16, 128)
    pieces = depth * ff // (16 * 128)

    def sixteen(*shape):
        return pltpu.VMEM(shape, kind)

    return pl.pallas_call(
        functools.partial(layer_kernel, experts),
        out_shape=[
            jax.ShapeDtypeStruct(tokens.shape, kind),
            jax.ShapeDtypeStruct((tok_rows, 1), jnp.float32),
        ]
        + [jax.ShapeDtypeStruct(block, jnp.float32)] * 4,
        in_specs=[VMEM] * 9 + [pl.BlockSpec(memory_space=pltpu.SMEM)],
        out_specs=[VMEM] * 6,
        scratch_shapes=[
            sixteen(HALVES, model, 2 * ff),
            sixteen(HALVES, model, ff),
            pltpu.VMEM((slots * model // lanes, lanes), jnp.float32),
            sixteen(slots, model),
            sixteen(slots, model),
            pltpu.VMEM((slots, 2 * ff), jnp.float32),
            sixteen(slots, ff),
        ]
        + [sixteen(*packed)] * 6
        + [
            sixteen(HALVES, RING * RING, CORES, *block),
            sixteen(HALVES, RING * RING, *block),
            sixteen(RING, HALVES, RING, *block),
            sixteen(RING - 1, HALVES, RING, *block),
            pltpu.VMEM((NODES,) + block, jnp.float32),
            sixteen(2, NODES // 2, *block),
            sixteen(2, NODES // 2, *block),
            sixteen(pieces, *piece),
            sixteen(experts, *piece),
            sixteen(experts, *piece),
            sixteen(pieces, *piece),
            dma((2,)),
        ]
        + [dma((hosts,))] * 6
        + ([dma((NODES,))] * 2 + [dma((NODES, RING - 1))] * 2 + [dma((NODES, RING))] * 2) * 2
        + [dma] * 2
        + [dma((NODES, RING - 1))] * 2
        + [dma((2, NODES // 2))] * 2
        + [dma((pieces,)), dma((experts,)), dma((experts,)), dma((pieces,))],
        compiler_params=pltpu.CompilerParams(
            collective_id=0, has_side_effects=True, vmem_limit_bytes=48 * 1024 * 1024
        ),
        name="layer",
    )(place_slots, place_slots.T, gates, tokens, cotangent, weight, *state, source)


def shards(
    tokens,
    route_ids,
    route_gates,
    cotangent,
    expert_weights,
    master,
    first_moment,
    second_moment,
    old_place,
    new_place,
):
    experts = lax.axis_size("expert")
    tok_rows = tokens.shape[0]
    routes = route_ids.shape[1]
    capacity = 5 * tok_rows * routes // (4 * experts)
    slots = experts * capacity
    expert_range = jnp.arange(experts, dtype=jnp.int32)
    holder = jnp.sum(
        expert_range[None, :] * (old_place[None, :] == expert_range[:, None]).astype(jnp.int32),
        axis=1,
    )
    flat_ids = route_ids.reshape(-1)
    onehot = (flat_ids[:, None] == expert_range[None, :]).astype(jnp.int32)
    rank_in = jnp.sum((jnp.cumsum(onehot, axis=0) - onehot) * onehot, axis=1)
    target = jnp.sum(onehot * holder[None, :], axis=1)
    slot_index = target * capacity + rank_in
    slot_range = jnp.arange(slots, dtype=jnp.int32)
    place_pairs = (slot_range[:, None] == slot_index[None, :]).astype(jnp.bfloat16)
    source_slot = jnp.sum(
        expert_range[None, :] * (old_place[None, :] == new_place[:, None]).astype(jnp.int32), axis=1
    )
    combined, gate_grads, *state = layer(
        place_pairs,
        route_gates,
        tokens,
        cotangent,
        expert_weights[0],
        (master[0], first_moment[0], second_moment[0]),
        source_slot,
    )
    return (combined, gate_grads) + tuple(value[None] for value in state)


def solution(mesh):
    in_specs = (
        P(("dp", "expert"), None),
        P(("dp", "expert"), None),
        P(("dp", "expert"), None),
        P(("dp", "expert"), None),
        P("expert", "dp", None),
        P("expert", "dp", None),
        P("expert", "dp", None),
        P("expert", "dp", None),
        P(),
        P(),
    )
    out_specs = (
        P(("dp", "expert"), None),
        P(("dp", "expert"), None),
        P("expert", "dp", None),
        P("expert", "dp", None),
        P("expert", "dp", None),
        P("expert", "dp", None),
    )
    return jax.shard_map(shards, mesh=mesh, in_specs=in_specs, out_specs=out_specs, check_vma=False)
```

```python
import functools

import jax
import jax.numpy as jnp
from jax import lax
from jax.experimental import pallas as pl
from jax.experimental.pallas import tpu as pltpu
from jax.sharding import PartitionSpec as P

beta_first = 0.9
beta_second = 0.999
learn_rate = 0.01
adam_eps = 1e-08

MESH = pl.DeviceIdType.MESH
VMEM = pl.BlockSpec(memory_space=pltpu.VMEM)
RING = 4
CORES = 2
HALVES = 2
NODES = RING * HALVES


def silu_value(values):
    return values * jax.nn.sigmoid(values)


def contract_rows(left, right):
    return lax.dot_general(
        left, right, (((0,), (0,)), ((), ())), preferred_element_type=jnp.float32
    )


def place():
    dp, ex = lax.axis_index("dp"), lax.axis_index("expert")
    return dp, ex, dp // (RING * CORES), (dp // CORES) % RING, dp % CORES


def index_of(z, y, core):
    return ((z % RING) * RING + y % RING) * CORES + core


def send(src, dst, send_sem, recv_sem, device):
    return pltpu.make_async_remote_copy(
        src_ref=src,
        dst_ref=dst,
        send_sem=send_sem,
        recv_sem=recv_sem,
        device_id=device,
        device_id_type=MESH,
    )


def greet(devices, experts, dp, ex):
    barrier = pltpu.get_barrier_semaphore()
    for device in devices:
        pl.semaphore_signal(barrier, inc=1, device_id=device, device_id_type=MESH)

    def one(step, carry):
        pl.semaphore_signal(
            barrier, inc=1, device_id=(dp, (ex + step) % experts), device_id_type=MESH
        )
        return carry

    lax.fori_loop(1, experts, one, 0)
    return lambda: pl.semaphore_wait(barrier, len(devices) + experts - 1)


def exchange(hosts, dp, ex, src, dst, send_sems, recv_sems):
    me, first = ex % hosts, ex - ex % hosts

    def copy(step):
        target = (me + step) % hosts
        return send(
            src.at[:, target],
            dst.at[:, me],
            send_sems.at[target],
            recv_sems.at[me],
            (dp, first + target),
        )

    def start(step, carry):
        copy(step).start()
        return carry

    def arrival(step, carry):
        other = (me + step) % hosts
        there = dst.at[:, other]
        send(
            there, there, send_sems.at[other], recv_sems.at[other], (dp, first + other)
        ).wait_recv()
        return carry

    def departure(step, carry):
        copy(step).wait_send()
        return carry

    lax.fori_loop(1, hosts, start, 0)
    for half in range(HALVES):
        dst[half, me] = src[half, me]
    return (
        lambda: lax.fori_loop(1, hosts, arrival, 0),
        lambda: lax.fori_loop(1, hosts, departure, 0),
    )


def middle(q, core):
    z = 2 + 2 * (q // RING)
    return (z + core * (7 - 2 * z)) * RING + q % RING


def middle_of(ex, core):
    z = ex // RING
    z = z + core * (7 - 2 * z)
    return (z % 2 == 0) & (z >= 2), (z // 2 - 1) * RING + ex % RING


def layer_kernel(
    experts,
    place_ref,
    pick_ref,
    gates_ref,
    tokens_ref,
    cot_ref,
    weight_ref,
    master_ref,
    first_ref,
    second_ref,
    source_ref,
    combined_ref,
    gate_grads_ref,
    grads_ref,
    new_master_ref,
    new_first_ref,
    new_second_ref,
    whole,
    whole_down,
    pack,
    rows,
    rows_up,
    both,
    hidden,
    in_from,
    in_to,
    up_from,
    up_to,
    out_from,
    out_to,
    partial,
    c_buf,
    y_from,
    y_buf,
    z_own,
    z_from,
    z_buf,
    state,
    spread,
    ordered,
    arrived,
    local_sem,
    in_send,
    in_recv,
    up_send,
    up_recv,
    out_send,
    out_recv,
    wz_send,
    wz_recv,
    wy_send,
    wy_recv,
    wc_send,
    wc_recv,
    dz_send,
    dz_recv,
    dy_send,
    dy_recv,
    dc_send,
    dc_recv,
    c_send,
    c_recv,
    y_send,
    y_recv,
    z_send,
    z_recv,
    s_send,
    s_recv,
    t_send,
    t_recv,
):
    dp, ex, z, y, core = place()
    sibling = (index_of(z, y, 1 - core), ex)
    ring_y = [(index_of(z, y + s, core), ex) for s in range(1, RING)]
    hosts = experts // HALVES
    node = z * HALVES + ex // hosts

    def at_node(step):
        other = (node + step + NODES) % NODES
        return (index_of(other // HALVES, y, core), other % HALVES * hosts + ex % hosts)

    right, left = at_node(1), at_node(-1)
    outer = at_node(2 * (ex // hosts) - 1)
    all_here = greet([sibling, outer] + ring_y, experts, dp, ex)

    slots, model = rows.shape
    depth = weight_ref.shape[0]
    ff = hidden.shape[1]
    lanes = pack.shape[1]
    per_row = model // lanes
    block = in_from.shape[2]
    part_rows = slots // HALVES
    quarter = model // RING
    group = per_row // RING

    def columns(i, width):
        return pl.ds(pl.multiple_of(i * width, width), width)

    def pack_columns(i, value):
        for c in range(group):
            pack[pl.ds(i * group + c, slots, stride=per_row), :] = value[
                :, c * lanes : (c + 1) * lanes
            ]

    def to_blocks(dst):
        for half in range(HALVES):
            value = pack[pl.ds(half * hosts * block, hosts * block), :].astype(dst.dtype)
            dst[half] = value.reshape((hosts, block, lanes))

    def to_rows(src, dst):
        for half in range(HALVES):
            value = src[half].astype(jnp.float32)
            pack[pl.ds(half * hosts * block, hosts * block), :] = value.reshape(
                (hosts * block, lanes)
            )

        def other(i, carry):
            for c in range(group):
                value = pack[pl.ds(i * group + c, slots, stride=per_row), :]
                dst[:, columns(i * group + c, lanes)] = value.astype(dst.dtype)
            return carry

        lax.fori_loop(0, RING, other, 0)

    def place_in(i, carry):
        value = tokens_ref[:, columns(i, quarter)]
        pack_columns(i, jnp.dot(place_ref[...], value, preferred_element_type=jnp.float32))
        return carry

    def place_up(i, carry):
        value = gates_ref[...] * cot_ref[:, columns(i, quarter)].astype(jnp.float32)
        value = value.astype(cot_ref.dtype)
        pack_columns(i, jnp.dot(place_ref[...], value, preferred_element_type=jnp.float32))
        return carry

    lax.fori_loop(0, RING, place_in, 0)
    to_blocks(in_from)
    all_here()

    sent = []

    def start(copy):
        copy.start()
        sent.append(copy)

    nodes = [(node + step + NODES) % NODES for step in (0, -1, 1, -2, 2, -3, 3, 4)]
    half = depth // 2
    every, low, high = (0, depth), (0, half), (half, half)

    def gather(src, dst, zs, zr, ys, yr, cs, cr):
        def slot(k, first=0, count=depth, y=y, core=core):
            row = index_of(nodes[k] // HALVES, y, core) * depth + first
            return dst.at[nodes[k] % HALVES, pl.ds(pl.multiple_of(row, half), count), :]

        def z_copy(i, from_ref, k, part, device):
            return send(from_ref, slot(k, *part), zs.at[i], zr.at[i], device)

        def z_arrival(i, k, part=every):
            there = slot(k, *part)
            send(there, there, zs.at[i], zr.at[i], right).wait_recv()

        def spread_weight(k, from_ref):
            for s in range(1, RING):
                start(
                    send(from_ref, slot(k), ys.at[k, s - 1], yr.at[k, s - 1], ring_y[s - 1])
                )
            start(send(from_ref, slot(k), cs.at[k, 0], cr.at[k, 0], sibling))

        def begin():
            start(z_copy(0, src, 0, every, right))
            start(z_copy(1, src, 0, every, left))

        def begin_across():
            spread_weight(0, src)

        def arrive(step):
            from_left, from_right = 2 * step - 1, 2 * step
            part = every if step < 3 else low
            z_arrival(2 * step - 2, from_left)
            start(z_copy(2 * step, slot(from_left, *part), from_left, part, right))
            part = every if step < 3 else high
            z_arrival(2 * step - 1, from_right)
            start(z_copy(2 * step + 1, slot(from_right, *part), from_right, part, left))
            spread_weight(from_left, slot(from_left))
            spread_weight(from_right, slot(from_right))

        def opposite():
            z_arrival(6, 7, low)
            z_arrival(7, 7, high)
            spread_weight(7, slot(7))

        def pass_on(k):
            for s in range(1, RING):
                there = slot(k, y=y + RING - s)
                send(there, there, ys.at[k, s - 1], yr.at[k, s - 1], sibling).wait_recv()
                start(send(there, there, cs.at[k, s], cr.at[k, s], sibling))

        def complete(k):
            for s in range(RING):
                there = slot(k, y=y + RING - s, core=1 - core)
                send(there, there, cs.at[k, s], cr.at[k, s], sibling).wait_recv()

        own = pltpu.make_async_copy(src, slot(0), local_sem.at[0 if dst is whole else 1])
        return own, begin, begin_across, arrive, opposite, pass_on, complete

    gate_up = gather(
        weight_ref.at[:, pl.ds(0, 2 * ff)],
        whole,
        wz_send,
        wz_recv,
        wy_send,
        wy_recv,
        wc_send,
        wc_recv,
    )
    down = gather(
        weight_ref.at[:, pl.ds(2 * ff, ff)],
        whole_down,
        dz_send,
        dz_recv,
        dy_send,
        dy_recv,
        dc_send,
        dc_recv,
    )
    own, begin, begin_across, arrive, opposite, pass_on, complete = gate_up
    begin()
    begin_across()
    in_there, in_left = exchange(hosts, dp, ex, in_from, in_to, in_send, in_recv)
    own.start()
    lax.fori_loop(0, RING, place_up, 0)
    to_blocks(up_from)
    both[...] = jnp.zeros_like(both)

    def rows_of(half):
        return pl.ds(pl.multiple_of(half * part_rows, part_rows), part_rows)

    def multiply(k):
        complete(k)
        half, part = nodes[k] % HALVES, columns(nodes[k] // HALVES, quarter)
        these = rows_of(half)
        both[these, :] += jnp.dot(
            rows[these, part], whole[half, part, :], preferred_element_type=jnp.float32
        )

    arrive(1)
    pass_on(0)
    arrive(2)
    up_there, up_left = exchange(hosts, dp, ex, up_from, up_to, up_send, up_recv)
    pass_on(1)
    pass_on(2)
    in_there()
    to_rows(in_to, rows)
    own.wait()
    arrive(3)
    pass_on(3)
    pass_on(4)
    multiply(0)
    multiply(1)
    multiply(2)
    opposite()
    begin_down = down[1]
    begin_down()
    pass_on(5)
    pass_on(6)
    multiply(3)
    multiply(4)
    multiply(5)
    multiply(6)
    pass_on(7)
    up_there()
    to_rows(up_to, rows_up)
    multiply(7)
    own, _, begin_across, arrive, opposite, pass_on, complete = down
    own.start()
    hidden[...] = (silu_value(both[:, :ff]) * both[:, ff:]).astype(hidden.dtype)

    def grad(i, carry):
        for half in range(HALVES):
            these = pl.ds(half * part_rows, part_rows)
            value = contract_rows(rows_up[these, columns(i, quarter)], hidden[these, :])
            partial[half, pl.ds(i * RING, RING)] = value.astype(partial.dtype).reshape(
                (RING, CORES, depth, ff)
            )
        return carry

    lax.fori_loop(0, RING, grad, 0)
    to_core = send(partial.at[:, :, 1 - core], c_buf, c_send, c_recv, sibling)
    to_core.start()
    to_core.wait()

    def pair(i, carry):
        at, row = i // RING, i % RING
        for half in range(HALVES):
            y_from[row, half, at] = (
                partial[half, i, core].astype(jnp.float32) + c_buf[half, i].astype(jnp.float32)
            ).astype(y_from.dtype)
        return carry

    lax.fori_loop(0, RING * RING, pair, 0)
    order = (4, 3, -3, 2, -2, 1, -1, 0)
    targets = [(node + step + NODES) % NODES for step in order]

    def y_copy(k, s):
        at = (targets[k] % HALVES, targets[k] // HALVES)
        return send(
            y_from.at[(y + s) % RING, at[0], at[1]],
            y_buf.at[s - 1, at[0], at[1]],
            y_send.at[k, s - 1],
            y_recv.at[k, s - 1],
            ring_y[s - 1],
        )

    for k in range(NODES):
        for s in range(1, RING):
            y_copy(k, s).start()
    begin_across()

    def y_sum(k):
        part, at = targets[k] % HALVES, targets[k] // HALVES
        total = y_from[y, part, at].astype(jnp.float32)
        for s in range(1, RING):
            y_copy(k, s).wait_recv()
            total += y_buf[s - 1, part, at].astype(jnp.float32)
        z_own[targets[k]] = total

    def mine(step):
        return z_own[(node + step + NODES) % NODES]

    def ring_copy(step, way):
        rows_sent = pl.ds(way * half, half) if step == 0 else pl.ds(0, depth)
        return send(
            z_from.at[way, step, rows_sent],
            z_buf.at[way, step, rows_sent],
            z_send.at[way, step],
            z_recv.at[way, step],
            (right, left)[way],
        )

    def ring_step(step):
        for way in range(2):
            total = mine((NODES // 2 - step) * (1 - 2 * way))
            if step == 0:
                cut = slice(way * half, way * half + half)
                z_from[way, step, cut, :] = total[cut].astype(z_from.dtype)
            elif step == 1:
                ring_copy(0, way).wait_recv()
                here, there = (0, half) if way == 0 else (half, 0)
                z_from[way, step, here : here + half, :] = (
                    total[here : here + half]
                    + z_buf[way, 0, here : here + half, :].astype(jnp.float32)
                ).astype(z_from.dtype)
                z_from[way, step, there : there + half, :] = total[there : there + half].astype(
                    z_from.dtype
                )
            else:
                ring_copy(step - 1, way).wait_recv()
                z_from[way, step] = (total + z_buf[way, step - 1].astype(jnp.float32)).astype(
                    z_from.dtype
                )
            ring_copy(step, way).start()

    last = NODES // 2 - 1
    y_sum(0)
    ring_step(0)
    arrive(1)
    pass_on(0)
    y_sum(1)
    y_sum(2)
    ring_step(1)
    arrive(2)
    y_sum(3)
    y_sum(4)
    ring_step(2)
    pass_on(1)
    pass_on(2)
    arrive(3)
    y_sum(5)
    y_sum(6)
    ring_step(3)
    pass_on(3)
    pass_on(4)
    opposite()
    pass_on(5)
    pass_on(6)
    y_sum(7)
    for way in range(2):
        ring_copy(last, way).wait_recv()
    grads = mine(0) + z_buf[0, last].astype(jnp.float32) + z_buf[1, last].astype(jnp.float32)
    grads_ref[...] = grads
    first = beta_first * first_ref[...] + (1.0 - beta_first) * grads
    second = beta_second * second_ref[...] + (1.0 - beta_second) * grads * grads
    updated = master_ref[...] - learn_rate * first / (jnp.sqrt(second) + adam_eps)
    tall, wide = state.shape[2:]
    pieces = state.shape[0]
    across = grads.shape[1] // wide

    def piece(q):
        return pl.ds(q // across * tall, tall), pl.ds(q % across * wide, wide)

    for i, value in enumerate((updated, first, second)):
        value = value.astype(state.dtype)
        for q in range(pieces):
            row, column = q // across * tall, q % across * wide
            state[q, i] = value[row : row + tall, column : column + wide]

    is_middle, held = middle_of(ex, core)

    def spread_copy(q):
        return send(
            state.at[q], spread.at[ex], s_send.at[q], s_recv.at[ex], (dp, middle(q, core))
        )

    def spread_start(step, carry):
        q = (ex + step) % pieces

        @pl.when(middle(q, core) != ex)
        def _():
            spread_copy(q).start()

        return carry

    lax.fori_loop(0, pieces, spread_start, 0)

    def order_copy(step):
        target = (ex + step) % experts
        return send(
            ordered.at[target], arrived.at[held], t_send.at[target], t_recv.at[held], (dp, target)
        )

    pass_on(7)
    for k in range(NODES):
        complete(k)
    own.wait()

    def outputs(i, carry):
        for part in range(HALVES):
            value = lax.dot_general(
                hidden[pl.ds(part * part_rows, part_rows), :],
                whole_down[part, columns(i, quarter), :],
                (((1,), (1,)), ((), ())),
                preferred_element_type=jnp.float32,
            )
            for c in range(group):
                first_row = part * part_rows * per_row + i * group + c
                pack[pl.ds(first_row, part_rows, stride=per_row), :] = value[
                    :, c * lanes : (c + 1) * lanes
                ]
        return carry

    lax.fori_loop(0, RING, outputs, 0)
    to_blocks(out_from)
    out_there, out_left = exchange(hosts, dp, ex, out_from, out_to, out_send, out_recv)

    @pl.when(is_middle)
    def _():
        spread[ex] = state[held]

        def landed(step, carry):
            other = (ex + step) % experts
            there = spread.at[other]
            send(there, there, s_send.at[0], s_recv.at[other], (dp, other)).wait_recv()
            return carry

        def pick(e, carry):
            ordered[e] = spread[source_ref[e]]
            return carry

        def start(step, carry):
            order_copy(step).start()
            return carry

        lax.fori_loop(1, experts, landed, 0)
        lax.fori_loop(0, experts, pick, 0)
        lax.fori_loop(1, experts, start, 0)
        arrived[held] = ordered[ex]

    out_there()
    to_rows(out_to, rows)

    def combine(i, total):
        part = columns(i, quarter)
        value = jnp.dot(pick_ref[...], rows[:, part], preferred_element_type=jnp.float32)
        combined_ref[:, part] = (gates_ref[...] * value).astype(combined_ref.dtype)
        return total + cot_ref[:, part].astype(jnp.float32) * value

    total = lax.fori_loop(
        0, RING, combine, jnp.zeros((tokens_ref.shape[0], quarter), jnp.float32)
    )
    gate_grads_ref[...] = jnp.sum(total, axis=1, keepdims=True)

    for q in range(pieces):
        there = arrived.at[q]

        @pl.when(middle(q, core) != ex)
        def _(q=q, there=there):
            spread_copy(q).wait_send()
            send(
                there, there, t_send.at[0], t_recv.at[q], (dp, middle(q, core))
            ).wait_recv()

    for q in range(pieces):
        for i, ref in enumerate((new_master_ref, new_first_ref, new_second_ref)):
            ref[piece(q)] = arrived[q, i].astype(ref.dtype)

    @pl.when(is_middle)
    def _():
        def sent(step, carry):
            order_copy(step).wait_send()
            return carry

        lax.fori_loop(1, experts, sent, 0)

    for copy in sent:
        copy.wait_send()
    for step in range(last + 1):
        for way in range(2):
            ring_copy(step, way).wait_send()
    for k in range(NODES):
        for s in range(1, RING):
            y_copy(k, s).wait_send()
    in_left()
    up_left()
    out_left()


def layer(place_slots, gates, tokens, cotangent, weight, state, source):
    slots, tok_rows = place_slots.shape
    model = tokens.shape[1]
    experts = source.shape[0]
    depth, ff = weight.shape[0], weight.shape[1] // 3
    dma = pltpu.SemaphoreType.DMA
    kind = tokens.dtype
    lanes = 128
    hosts = experts // HALVES
    packed = (HALVES, hosts, slots * model // lanes // experts, lanes)
    block = (depth, ff)
    piece = (3, 16, 128)
    pieces = depth * ff // (16 * 128)

    def sixteen(*shape):
        return pltpu.VMEM(shape, kind)

    return pl.pallas_call(
        functools.partial(layer_kernel, experts),
        out_shape=[
            jax.ShapeDtypeStruct(tokens.shape, kind),
            jax.ShapeDtypeStruct((tok_rows, 1), jnp.float32),
        ]
        + [jax.ShapeDtypeStruct(block, jnp.float32)] * 4,
        in_specs=[VMEM] * 9 + [pl.BlockSpec(memory_space=pltpu.SMEM)],
        out_specs=[VMEM] * 6,
        scratch_shapes=[
            sixteen(HALVES, model, 2 * ff),
            sixteen(HALVES, model, ff),
            pltpu.VMEM((slots * model // lanes, lanes), jnp.float32),
            sixteen(slots, model),
            sixteen(slots, model),
            pltpu.VMEM((slots, 2 * ff), jnp.float32),
            sixteen(slots, ff),
        ]
        + [sixteen(*packed)] * 6
        + [
            sixteen(HALVES, RING * RING, CORES, *block),
            sixteen(HALVES, RING * RING, *block),
            sixteen(RING, HALVES, RING, *block),
            sixteen(RING - 1, HALVES, RING, *block),
            pltpu.VMEM((NODES,) + block, jnp.float32),
            sixteen(2, NODES // 2, *block),
            sixteen(2, NODES // 2, *block),
            sixteen(pieces, *piece),
            sixteen(experts, *piece),
            sixteen(experts, *piece),
            sixteen(pieces, *piece),
            dma((2,)),
        ]
        + [dma((hosts,))] * 6
        + ([dma((NODES,))] * 2 + [dma((NODES, RING - 1))] * 2 + [dma((NODES, RING))] * 2) * 2
        + [dma] * 2
        + [dma((NODES, RING - 1))] * 2
        + [dma((2, NODES // 2))] * 2
        + [dma((pieces,)), dma((experts,)), dma((experts,)), dma((pieces,))],
        compiler_params=pltpu.CompilerParams(
            collective_id=0, has_side_effects=True, vmem_limit_bytes=48 * 1024 * 1024
        ),
        name="layer",
    )(place_slots, place_slots.T, gates, tokens, cotangent, weight, *state, source)


def shards(
    tokens,
    route_ids,
    route_gates,
    cotangent,
    expert_weights,
    master,
    first_moment,
    second_moment,
    old_place,
    new_place,
):
    experts = lax.axis_size("expert")
    tok_rows = tokens.shape[0]
    routes = route_ids.shape[1]
    capacity = 5 * tok_rows * routes // (4 * experts)
    slots = experts * capacity
    expert_range = jnp.arange(experts, dtype=jnp.int32)
    holder = jnp.sum(
        expert_range[None, :] * (old_place[None, :] == expert_range[:, None]).astype(jnp.int32),
        axis=1,
    )
    flat_ids = route_ids.reshape(-1)
    onehot = (flat_ids[:, None] == expert_range[None, :]).astype(jnp.int32)
    rank_in = jnp.sum((jnp.cumsum(onehot, axis=0) - onehot) * onehot, axis=1)
    target = jnp.sum(onehot * holder[None, :], axis=1)
    slot_index = target * capacity + rank_in
    slot_range = jnp.arange(slots, dtype=jnp.int32)
    place_pairs = (slot_range[:, None] == slot_index[None, :]).astype(jnp.bfloat16)
    source_slot = jnp.sum(
        expert_range[None, :] * (old_place[None, :] == new_place[:, None]).astype(jnp.int32), axis=1
    )
    combined, gate_grads, *state = layer(
        place_pairs,
        route_gates,
        tokens,
        cotangent,
        expert_weights[0],
        (master[0], first_moment[0], second_moment[0]),
        source_slot,
    )
    return (combined, gate_grads) + tuple(value[None] for value in state)


def solution(mesh):
    in_specs = (
        P(("dp", "expert"), None),
        P(("dp", "expert"), None),
        P(("dp", "expert"), None),
        P(("dp", "expert"), None),
        P("expert", "dp", None),
        P("expert", "dp", None),
        P("expert", "dp", None),
        P("expert", "dp", None),
        P(),
        P(),
    )
    out_specs = (
        P(("dp", "expert"), None),
        P(("dp", "expert"), None),
        P("expert", "dp", None),
        P("expert", "dp", None),
        P("expert", "dp", None),
        P("expert", "dp", None),
    )
    return jax.shard_map(shards, mesh=mesh, in_specs=in_specs, out_specs=out_specs, check_vma=False)
```
